128 devices in a mesh: section: 2 (over y_lo), shard: 2 (over y_hi), rep: 32 (over z, x, core).
Axes of the slice: x: 4, y: 4 (y_hi: 2, y_lo: 2; y = y_hi * 2 + y_lo), z: 4, core: 2. Of those that a mesh axis runs over, the one named last changes fastest.
Arguments:
- tokens: bfloat16 [14336, 960], P(('shard', 'rep')), may hold values from -6 to 6
- segments: int32 [128, 112], P(('shard', 'rep')), may hold values from 0 to 2, as said below
- cotangent: float32 [14336, 960], P(('shard', 'rep')), may hold values from -6 to 6
- qkv_weight: bfloat16 [2, 960, 1600], P('section', 'shard'), may hold values from -0.1875 to 0.1875
- output_weight: bfloat16 [2, 960, 960], P('section', 'shard'), may hold values from -0.75 to 0.75
- gateup_weight: bfloat16 [2, 960, 5120], P('section', 'shard'), may hold values from -0.1875 to 0.1875
- down_weight: bfloat16 [2, 2560, 960], P('section', 'shard'), may hold values from -0.125 to 0.125
- norm_gains: bfloat16 [2, 2, 960], P('section', None, 'shard'), may hold values from 0.099609375 to 1.8984375
Outputs:
- activations: float32 [2, 14336, 960], P('section', ('shard', 'rep'))
- input_grads: float32 [2, 14336, 960], P('section', ('shard', 'rep'))
- qkv_grad: float32 [2, 960, 1600], P('section', ('shard', 'rep'))
- output_grad: float32 [2, 960, 960], P('section', ('shard', 'rep'))
- gateup_grad: float32 [2, 960, 5120], P('section', ('shard', 'rep'))
- down_grad: float32 [2, 2560, 960], P('section', ('shard', 'rep'))
- gains_grad: float32 [2, 2, 960], P('section', None, ('shard', 'rep'))
The draws below stay inside these ranges and needn't reach their ends.
Inputs may be any that keep to these rules, and one draw needn't show every extreme that they name: `segments`: within each row, numbers never fall and each of the 3 numbers covers at least one position; in every row exactly one number covers 84 positions, and the other two share the remaining 112 - 84 positions.
All inputs are finite; a program needn't handle non-finite values.
Results may differ from the reference program's by a relative error of at most 0.03.
Values may be sent and summed in bfloat16 or wider, within the bound.
No kernel may reach another device: no remote copies, remote signals or barrier semaphores. Data moves between devices by JAX's collectives and lax.ppermute only.
A program may use at most 256 MiB of HBM per device.

```python
import jax
import jax.numpy as jnp
from jax import lax

D = 960
HEADS = 15
KV_HEADS = 5
HEAD = 64
FF = 2560
LAYERS = 2
MB_ROWS = 112
SEQ_MOST = 84
TOKENS = 14336
QKV = 1600


def draw_segments(key, part):
    key = jax.random.fold_in(key, 5)
    row_count = TOKENS // MB_ROWS
    remaining = MB_ROWS - SEQ_MOST
    split_key, place_key = jax.random.split(key)
    first_short = jax.random.randint(split_key, (row_count,), 1, remaining, dtype=jnp.int32)
    second_short = remaining - first_short
    placing = jax.random.randint(place_key, (row_count,), 0, 3, dtype=jnp.int32)
    longest = jnp.full((row_count,), SEQ_MOST, jnp.int32)
    length_zero = jnp.where(placing == 0, longest, first_short)
    length_one = jnp.where(placing == 0, first_short, jnp.where(placing == 1, longest, second_short))
    end_zero = length_zero
    end_one = length_zero + length_one
    column = jnp.arange(MB_ROWS, dtype=jnp.int32)[None, :]
    return (column >= end_zero[:, None]).astype(jnp.int32) + (column >= end_one[:, None]).astype(jnp.int32)


def steps_of(rng, dims, pieces, low, largest):
    loudness = 1.0
    for position, shards_of in pieces:
        heights = jax.random.uniform(jax.random.fold_in(jax.random.fold_in(rng, 6), position), (shards_of,), jnp.float32, low / len(pieces), largest / len(pieces))
        loudness = loudness * jnp.repeat(jnp.exp(heights), dims[position] // shards_of).reshape((-1,) + (1,) * (len(dims) - 1 - position))
    return loudness


def centred(key, dims, width, limit, shards=(), kind=jnp.bfloat16):
    drawn = jax.random.normal(key, dims, jnp.float32) * width
    if len(shards) > 0:
        drawn = steps_of(key, dims, shards, -0.22, 0.18) * drawn
    return jnp.clip(drawn, min=-limit, max=limit).astype(kind)


def setup_inputs(seed: int = 0) -> dict:
    key_of = jax.random.split(jax.random.key(seed), 9)
    return {
        "tokens": centred(key_of[0], (TOKENS, D), 1.0, 6.0, ((0, 64),)),
        "segments": draw_segments(jax.random.fold_in(key_of[8], 71), 0),
        "cotangent": centred(key_of[2], (TOKENS, D), 1.0, 6.0, ((0, 64),), jnp.float32),
        "qkv_weight": centred(key_of[3], (LAYERS, D, QKV), D ** -0.5, 0.1875, ((0, 2), (1, 2))),
        "output_weight": centred(key_of[4], (LAYERS, HEADS * HEAD, D), (HEADS * HEAD // 16) ** -0.5, 0.75, ((0, 2), (1, 2))),
        "gateup_weight": centred(key_of[5], (LAYERS, D, 2 * FF), D ** -0.5, 0.1875, ((0, 2), (1, 2))),
        "down_weight": centred(key_of[6], (LAYERS, FF, D), FF ** -0.5, 0.125, ((0, 2), (1, 2))),
        "norm_gains": jnp.clip(1.0 + 0.18 * jax.random.normal(key_of[7], (LAYERS, 2, D), jnp.float32), 0.099609375, 1.8984375).astype(jnp.bfloat16),
    }


EPSILON = 1e-05
ROPE_BASE = 100000.0
NEGATIVE = -1e+30

@jax.custom_vjp
def low(v):
    return lax.optimization_barrier(v.astype(jnp.bfloat16)).astype(jnp.float32)

@jax.custom_vjp
def low_back(v):
    return v

def low_keep(v):
    return (low(v), None)

def low_pass(kept, grad):
    return (grad,)

def back_keep(v):
    return (v, None)

def back_low(kept, grad):
    return (low(grad),)
low.defvjp(low_keep, low_pass)
low_back.defvjp(back_keep, back_low)

def positions(labels):
    row_count = labels.shape[0]
    earlier = lax.optimization_barrier(jnp.sum((labels[None, :] < labels[:, None]).astype(jnp.int32), axis=1))
    return (jnp.arange(row_count, dtype=jnp.int32) - earlier).astype(jnp.float32)

def tables(labels):
    half_width = HEAD // 2
    frequency = ROPE_BASE ** (-jnp.arange(half_width, dtype=jnp.float32) * 2.0 / HEAD)
    angles = positions(labels)[:, None] * frequency[None, :]
    return (jnp.cos(angles)[:, None, :], jnp.sin(angles)[:, None, :])

def rotate(values, cosine_table, sine_table):
    half_width = values.shape[-1] // 2
    first_half = values[..., :half_width]
    second_half = values[..., half_width:]
    return jnp.concatenate([first_half * cosine_table - second_half * sine_table, second_half * cosine_table + first_half * sine_table], axis=-1)

def visible(labels):
    row_count = labels.shape[0]
    row_order = jnp.arange(row_count, dtype=jnp.int32)
    return (labels[:, None] == labels[None, :]) & (row_order[None, :] <= row_order[:, None])

def decoder_layer(stream, gains, qkv_full, out_full, gateup_full, down_full, labels):
    highest = lax.Precision.HIGHEST
    row_count = stream.shape[0]
    block_count, block_rows = labels.shape
    group_size = HEADS // KV_HEADS
    query_width = HEADS * HEAD
    key_width = KV_HEADS * HEAD
    head_scale = HEAD ** (-0.5)
    first_scale = lax.rsqrt(lax.optimization_barrier(jnp.mean(stream * stream, axis=-1, keepdims=True)) + EPSILON)
    attn_norm = low(stream * first_scale * gains[0])
    projected = low_back(jnp.dot(attn_norm, qkv_full, precision=highest))
    cosine_table, sine_table = jax.vmap(tables)(labels)
    cosine_table = cosine_table.reshape(row_count, 1, HEAD // 2)
    sine_table = sine_table.reshape(row_count, 1, HEAD // 2)
    query_heads = low(rotate(projected[:, :query_width].reshape(row_count, HEADS, HEAD), cosine_table, sine_table))
    key_heads = low(rotate(projected[:, query_width:query_width + key_width].reshape(row_count, KV_HEADS, HEAD), cosine_table, sine_table))
    value_heads = low(projected[:, query_width + key_width:].reshape(row_count, KV_HEADS, HEAD))

    def attend(block_data):
        block_query, block_key, block_value, block_labels = block_data
        scores = low_back(jnp.einsum('qkge,ske->kgqs', block_query, block_key, precision=highest) * head_scale)
        masked = jnp.where(visible(block_labels)[None, None], scores, NEGATIVE)
        maximum = lax.optimization_barrier(jnp.max(masked, axis=-1, keepdims=True))
        exponent = jnp.exp(masked - maximum)
        probability = exponent / lax.optimization_barrier(jnp.sum(exponent, axis=-1, keepdims=True))
        return jnp.einsum('kgqs,ske->qkge', low(probability), block_value, precision=highest)
    mixed_heads = lax.map(jax.checkpoint(attend), (query_heads.reshape(block_count, block_rows, KV_HEADS, group_size, HEAD), key_heads.reshape(block_count, block_rows, KV_HEADS, HEAD), value_heads.reshape(block_count, block_rows, KV_HEADS, HEAD), labels))
    mixed_heads = low(low_back(mixed_heads.reshape(row_count, query_width)))
    middle = stream + low_back(jnp.dot(mixed_heads, out_full, precision=highest))
    second_scale = lax.rsqrt(lax.optimization_barrier(jnp.mean(middle * middle, axis=-1, keepdims=True)) + EPSILON)
    ffn_norm = low(middle * second_scale * gains[1])
    gateup = low_back(jnp.dot(ffn_norm, gateup_full, precision=highest))
    gate_part = gateup[:, :FF]
    upward = gateup[:, FF:]
    hidden = low(gate_part * jax.nn.sigmoid(gate_part) * upward)
    return middle + low_back(jnp.dot(hidden, down_full, precision=highest))

def reference(tokens, segments, cotangent, qkv_weight, output_weight, gateup_weight, down_weight, norm_gains):
    start_stream = tokens.astype(jnp.float32)

    def layer_params(index):
        return (norm_gains[index].astype(jnp.float32), qkv_weight[index].astype(jnp.float32), output_weight[index].astype(jnp.float32), gateup_weight[index].astype(jnp.float32), down_weight[index].astype(jnp.float32))

    def section_layer(stream, gains, qkv_full, out_full, gateup_full, down_full):
        return decoder_layer(stream, gains, qkv_full, out_full, gateup_full, down_full, segments)
    first_out, first_pull = jax.vjp(section_layer, start_stream, *layer_params(0))
    second_out, second_pull = jax.vjp(section_layer, first_out, *layer_params(1))
    second_grads = second_pull(cotangent.astype(jnp.float32))
    first_grads = first_pull(second_grads[0])
    activations = jnp.stack([first_out, second_out])
    input_grads = jnp.stack([first_grads[0], second_grads[0]])
    gains_grad = jnp.stack([first_grads[1], second_grads[1]])
    qkv_grad = jnp.stack([first_grads[2], second_grads[2]])
    output_grad = jnp.stack([first_grads[3], second_grads[3]])
    gateup_grad = jnp.stack([first_grads[4], second_grads[4]])
    down_grad = jnp.stack([first_grads[5], second_grads[5]])
    return (activations, input_grads, qkv_grad, output_grad, gateup_grad, down_grad, gains_grad)
```

```python
import functools

import jax
import jax.numpy as jnp
import numpy as np
from jax import lax
from jax.experimental import pallas as pl
from jax.experimental.pallas import tpu as pltpu
from jax.sharding import Mesh
from jax.sharding import PartitionSpec as P

D = 960
HEADS = 15
KV_HEADS = 5
GROUP = HEADS // KV_HEADS
HEAD = 64
FF = 2560
QKV = 1600
ROWS = 112
LANES = 128
BLOCKS = 13
EPSILON = 1e-05
ROPE_BASE = 100000.0
NEGATIVE = -1e30
HEAD_SCALE = HEAD ** (-0.5)
BF16 = jnp.bfloat16
F32 = jnp.float32
REP = ("z", "x", "core")
SWAP = [(0, 1), (1, 0)]
VMEM_LIMIT = 48 * 1024 * 1024


def lane_ids(rows):
    return lax.broadcasted_iota(jnp.int32, (rows, LANES), 1)


def swapped_halves(x, low_half):
    return jnp.where(low_half, pltpu.roll(x, LANES - 32, 1), pltpu.roll(x, 32, 1))


def block_of(ref, index, width):
    start = index * LANES
    stop = min(start + LANES, width)
    part = ref[:, start:stop]
    if stop - start < LANES:
        part = jnp.concatenate([part, jnp.zeros((part.shape[0], LANES - (stop - start)), part.dtype)], axis=1)
    return part


def both_halves(block, slot, left):
    if slot == 0:
        low = jnp.where(left, block, 0.0)
        high = pltpu.roll(low, HEAD, 1)
    else:
        high = jnp.where(left, 0.0, block)
        low = pltpu.roll(high, HEAD, 1)
    return low.astype(BF16), high.astype(BF16)


def contract(a, b, dims):
    return lax.dot_general(a, b, ((dims[0:1], dims[1:2]), ((), ())), preferred_element_type=F32)


def attend_kernel(proj_ref, mask_ref, cos_ref, sin_ref, heads_ref, prob_ref, mixed_ref):
    lanes = lane_ids(ROWS)
    left = lanes < HEAD
    low_half = (lanes % HEAD) < 32
    cos = cos_ref[...]
    sin = sin_ref[...]
    mask = mask_ref[0] > 0.0
    blocks = []
    for b in range(BLOCKS):
        x = block_of(proj_ref, b, QKV)
        if b < 10:
            x = x * cos + swapped_halves(x, low_half) * sin
        low = x.astype(BF16)
        blocks.append(low)
        stop = min(b * LANES + LANES, QKV)
        heads_ref[:, b * LANES : stop] = low[:, : stop - b * LANES]
    mixed = [None] * 8
    for kk in range(KV_HEADS):
        kslot, vslot = HEADS + kk, HEADS + KV_HEADS + kk
        keys = both_halves(blocks[kslot // 2].astype(F32), kslot % 2, left)
        values = both_halves(blocks[vslot // 2].astype(F32), vslot % 2, left)
        for h in range(kk * GROUP, kk * GROUP + GROUP):
            half, b = h % 2, h // 2
            scores = contract(keys[half], blocks[b], (1, 1)) * HEAD_SCALE
            scores = jnp.where(mask, scores, NEGATIVE)
            top = jnp.max(scores, axis=0, keepdims=True)
            raised = jnp.exp(scores - top)
            prob = raised / jnp.sum(raised, axis=0, keepdims=True)
            prob_ref[0, h] = prob
            part = contract(prob.astype(BF16), values[half], (0, 0))
            mixed[b] = part if mixed[b] is None else mixed[b] + part
    for b in range(8):
        stop = min(b * LANES + LANES, D)
        mixed_ref[:, b * LANES : stop] = mixed[b].astype(BF16)[:, : stop - b * LANES]


def attend_back_kernel(heads_ref, prob_ref, dmixed_ref, cos_ref, sin_ref, out_ref):
    lanes = lane_ids(ROWS)
    left = lanes < HEAD
    low_half = (lanes % HEAD) < 32
    cos = cos_ref[...]
    sin = sin_ref[...]
    blocks = [block_of(heads_ref, b, QKV) for b in range(BLOCKS)]
    dmixed = [block_of(dmixed_ref, b, D) for b in range(8)]
    outs = [None] * BLOCKS

    def add(index, term):
        outs[index] = term if outs[index] is None else outs[index] + term

    for kk in range(KV_HEADS):
        kslot, vslot = HEADS + kk, HEADS + KV_HEADS + kk
        keys = both_halves(blocks[kslot // 2].astype(F32), kslot % 2, left)
        values = both_halves(blocks[vslot // 2].astype(F32), vslot % 2, left)
        dkeys = [None, None]
        dvalues = [None, None]
        for h in range(kk * GROUP, kk * GROUP + GROUP):
            half, b = h % 2, h // 2
            prob = prob_ref[0, h]
            dprob = contract(values[half], dmixed[b], (1, 1))
            inner = jnp.sum(dprob * prob, axis=0, keepdims=True)
            dscore = (prob * (dprob - inner)).astype(BF16)
            add(b, contract(dscore, keys[half], (0, 0)))
            dk = contract(dscore, blocks[b], (1, 0))
            dv = contract(prob.astype(BF16), dmixed[b], (1, 0))
            dkeys[half] = dk if dkeys[half] is None else dkeys[half] + dk
            dvalues[half] = dv if dvalues[half] is None else dvalues[half] + dv
        for slot, (low, high) in ((kslot, dkeys), (vslot, dvalues)):
            low = jnp.where(left, low, 0.0)
            high = jnp.where(left, 0.0, high)
            if slot % 2 == 0:
                term = low + pltpu.roll(high, HEAD, 1)
            else:
                term = pltpu.roll(low, HEAD, 1) + high
            add(slot // 2, term)
    for b in range(BLOCKS):
        x = outs[b]
        if b < 10:
            x = x * HEAD_SCALE
            x = x * cos - swapped_halves(x, low_half) * sin
        stop = min(b * LANES + LANES, QKV)
        out_ref[:, b * LANES : stop] = x.astype(BF16)[:, : stop - b * LANES]


def row_spec(width):
    return pl.BlockSpec((ROWS, width), lambda i: (i, 0))


def attend(projected, mask, cos, sin):
    count = mask.shape[0]
    rows = count * ROWS
    return pl.pallas_call(
        attend_kernel,
        grid=(count,),
        in_specs=[
            row_spec(QKV),
            pl.BlockSpec((1, ROWS, ROWS), lambda i: (i, 0, 0)),
            row_spec(LANES),
            row_spec(LANES),
        ],
        out_specs=[
            row_spec(QKV),
            pl.BlockSpec((1, HEADS, ROWS, ROWS), lambda i: (i, 0, 0, 0)),
            row_spec(D),
        ],
        out_shape=[
            jax.ShapeDtypeStruct((rows, QKV), BF16),
            jax.ShapeDtypeStruct((count, HEADS, ROWS, ROWS), F32),
            jax.ShapeDtypeStruct((rows, D), BF16),
        ],
        compiler_params=pltpu.CompilerParams(vmem_limit_bytes=VMEM_LIMIT),
        name="attend",
    )(projected, mask, cos, sin)


def attend_back(heads, prob, dmixed, cos, sin):
    count = prob.shape[0]
    rows = count * ROWS
    return pl.pallas_call(
        attend_back_kernel,
        grid=(count,),
        in_specs=[
            row_spec(QKV),
            pl.BlockSpec((1, HEADS, ROWS, ROWS), lambda i: (i, 0, 0, 0)),
            row_spec(D),
            row_spec(LANES),
            row_spec(LANES),
        ],
        out_specs=row_spec(QKV),
        out_shape=jax.ShapeDtypeStruct((rows, QKV), BF16),
        compiler_params=pltpu.CompilerParams(vmem_limit_bytes=VMEM_LIMIT),
        name="attend_back",
    )(heads, prob, dmixed, cos, sin)


def tables(segments):
    count, rows = segments.shape
    earlier = jnp.sum((segments[:, None, :] < segments[:, :, None]).astype(jnp.int32), axis=2)
    position = (jnp.arange(rows, dtype=jnp.int32)[None, :] - earlier).astype(F32).reshape(count * rows, 1)
    frequency = ROPE_BASE ** (-jnp.arange(HEAD // 2, dtype=F32) * 2.0 / HEAD)
    angles = position * frequency[None, :]
    cos, sin = jnp.cos(angles), jnp.sin(angles)
    order = jnp.arange(rows, dtype=jnp.int32)
    mask = (segments[:, :, None] == segments[:, None, :]) & (order[:, None] <= order[None, :])[None]
    return (
        jnp.concatenate([cos] * 4, axis=1),
        jnp.concatenate([-sin, sin, -sin, sin], axis=1),
        mask.astype(F32),
    )


def mm(a, b):
    return jnp.dot(a, b, preferred_element_type=F32)


def mmt(a, b):
    return lax.dot_general(a, b, (((1,), (1,)), ((), ())), preferred_element_type=F32)


def halves(x, first):
    cut = x.shape[1] // 2
    own = jnp.where(first, x[:, :cut], x[:, cut:])
    other = jnp.where(first, x[:, cut:], x[:, :cut])
    if cut == 480:
        other = jnp.pad(other, ((0, 0), (0, 32)))
    return own, other


def times(x, weight, first):
    own, other = halves(x, first)
    return mm(own, weight[0]) + mm(other, weight[1])


def times_back(x, weight, first):
    own, other = mmt(x, weight[0]), mmt(x, weight[1])[:, : weight[0].shape[0]]
    return jnp.concatenate([jnp.where(first, own, other), jnp.where(first, other, own)], axis=1)


def layer_forward(stream, first, gains, weights, table):
    qkv_w, out_w, gateup_w, down_w = weights
    cos, sin, mask = table
    first_scale = lax.rsqrt(jnp.mean(stream * stream, axis=-1, keepdims=True) + EPSILON)
    attn_norm = (stream * first_scale * gains[0]).astype(BF16)
    projected = times(attn_norm, qkv_w, first)
    heads, prob, mixed = attend(projected, mask, cos, sin)
    middle = stream + times(mixed, out_w, first)
    second_scale = lax.rsqrt(jnp.mean(middle * middle, axis=-1, keepdims=True) + EPSILON)
    ffn_norm = (middle * second_scale * gains[1]).astype(BF16)
    gateup = times(ffn_norm, gateup_w, first)
    gate, up = gateup[:, :FF], gateup[:, FF:]
    hidden = (gate * jax.nn.sigmoid(gate) * up).astype(BF16)
    output = middle + times(hidden, down_w, first)
    return output, (stream, first_scale, attn_norm, heads, prob, mixed, middle, second_scale, ffn_norm, gate, up, hidden)


def norm_back(incoming, gain, scale, normed):
    scaled = incoming * gain
    return scale * (scaled - normed * jnp.mean(scaled * normed, axis=-1, keepdims=True))


def layer_backward(dy, kept, first, gains, weights, table, grads):
    qkv_w, out_w, gateup_w, down_w = weights
    cos, sin, _ = table
    stream, first_scale, attn_norm, heads, prob, mixed, middle, second_scale, ffn_norm, gate, up, hidden = kept
    dz = dy.astype(BF16)
    if grads is not None:
        grads.down(hidden, dz)
    dhidden = times_back(dz, down_w, first)
    s = jax.nn.sigmoid(gate)
    dgateup = jnp.concatenate(
        [dhidden * up * s * (1.0 + gate * (1.0 - s)), dhidden * gate * s], axis=1
    ).astype(BF16)
    if grads is not None:
        grads.rows("gateup", ffn_norm, dgateup)
    dffn = times_back(dgateup, gateup_w, first)
    second_normed = middle * second_scale
    dmiddle = dy + norm_back(dffn, gains[1], second_scale, second_normed)
    dbranch = dmiddle.astype(BF16)
    if grads is not None:
        grads.rows("output", mixed, dbranch)
    dmixed = times_back(dbranch, out_w, first).astype(BF16)
    dprojected = attend_back(heads, prob, dmixed, cos, sin)
    dattn = times_back(dprojected, qkv_w, first)
    first_normed = stream * first_scale
    if grads is not None:
        gain_grads = jnp.stack([jnp.sum(dattn * first_normed, axis=0), jnp.sum(dffn * second_normed, axis=0)], axis=1)
        grads.rows("qkv", attn_norm, dprojected, gain_grads)
    return dmiddle + norm_back(dattn, gains[0], first_scale, first_normed)


def row_order():
    pick = np.zeros((D, 1024), np.float32)
    for row in range(D):
        s, rest = divmod(row, 480)
        chunk, i = divmod(rest, 30)
        pick[row, chunk * 64 + s * 32 + i] = 1.0
    return pick


class Gradients:
    def __init__(self):
        self.core = lax.axis_index("core") == 0
        self.shard = lax.axis_index("shard") == 0
        self.pick = jnp.asarray(row_order(), BF16)
        self.found = {}

    def shared(self, left, right):
        cut = right.shape[1] // 2
        keep = jnp.where(self.core, right[:, :cut], right[:, cut:])
        give = jnp.where(self.core, right[:, cut:], right[:, :cut])
        left_other = lax.ppermute(left, "core", SWAP)
        right_other = lax.ppermute(give, "core", SWAP)
        return jnp.concatenate([left, left_other], axis=0), jnp.concatenate([keep, right_other], axis=0)

    def scatter(self, value):
        return lax.psum_scatter(value, ("z", "x"), scatter_dimension=0, tiled=True)

    def joined(self, piece, per_core):
        columns = piece.shape[1]
        parts = piece.reshape(2, 2, per_core, columns)
        by_shard = jnp.where(self.shard, parts, parts[::-1])
        by_both = jnp.where(self.core, by_shard, by_shard[:, ::-1])
        axes = ("shard", "core")
        across = lax.ppermute(by_both[1, 0], axes, [(0, 2), (2, 0), (1, 3), (3, 1)]).astype(F32)
        beside = lax.ppermute(by_both[0, 1], axes, [(0, 1), (1, 0), (2, 3), (3, 2)]).astype(F32)
        corner = lax.ppermute(by_both[1, 1], axes, [(0, 3), (3, 0), (1, 2), (2, 1)]).astype(F32)
        own = by_both[0, 0].astype(F32) + across
        other = beside + corner
        return jnp.where(self.core, own, other), jnp.where(self.core, other, own)

    def down(self, hidden, dz):
        left, right = self.shared(hidden, dz)
        made = [
            lax.dot_general(part, right, (((0,), (0,)), ((), ())), preferred_element_type=F32).astype(BF16)
            for part in (left[:, : FF // 2], left[:, FF // 2 :])
        ]
        whole = jnp.stack([m.reshape(16, 80, 480) for m in made], axis=1).reshape(FF, 480)
        self.found["down"] = jnp.concatenate(self.joined(self.scatter(whole), 40), axis=1)[None]

    def rows(self, name, left, right, extra=None):
        picked = mm(left, self.pick).astype(BF16)
        left, right = self.shared(picked, right)
        whole = lax.dot_general(left, right, (((0,), (0,)), ((), ())), preferred_element_type=F32).astype(BF16)
        width = whole.shape[1]
        if extra is not None:
            extra = lax.dot_general(self.pick, extra.astype(BF16), (((0,), (0,)), ((), ())), preferred_element_type=F32)
            whole = jnp.concatenate([whole, extra.astype(BF16)], axis=1)
        piece = self.scatter(whole)
        piece = piece.reshape(2, 32, piece.shape[1])[:, :30].reshape(60, piece.shape[1])
        low, high = self.joined(piece, 15)
        self.found[name] = jnp.concatenate([low[:, :width], high[:, :width]], axis=1)[None]
        if extra is not None:
            self.found["gains"] = (low[:, width:] + high[:, width:]).T[None]


def shards(tokens, segments, cotangent, qkv_weight, output_weight, gateup_weight, down_weight, norm_gains):
    leading = lax.axis_index("section") == 0
    first = lax.axis_index("shard") == 0
    rep = lax.axis_index(REP)

    owned = (qkv_weight[0], output_weight[0], gateup_weight[0])
    start = jnp.minimum(rep * 16, 464)
    slices = jnp.concatenate([lax.dynamic_slice_in_dim(w, start, 16, 0) for w in owned], axis=1)
    slices = lax.ppermute(slices, "shard", SWAP)
    down_slice = lax.ppermute(lax.dynamic_slice_in_dim(down_weight[0], rep * 40, 40, 0), "shard", SWAP)
    other_gains = lax.ppermute(norm_gains[0], "shard", SWAP)
    own_gains = norm_gains[0]
    gains = jnp.concatenate(
        [jnp.where(first, own_gains, other_gains), jnp.where(first, other_gains, own_gains)], axis=1
    ).astype(F32)
    weights, at = [], 0
    for w in owned:
        piece = slices[:, at : at + w.shape[1]]
        at += w.shape[1]
        weights.append((w, lax.all_gather(piece, REP, axis=0, tiled=True)))
    weights.append((down_weight[0], lax.all_gather(down_slice, REP, axis=0, tiled=True)))

    table = tables(segments)
    inputs = tokens.astype(F32)
    early, _ = layer_forward(inputs, first, gains, weights, table)
    arrived = lax.ppermute(early.astype(BF16), "section", [(0, 1)]).astype(F32)
    stream = jnp.where(leading, inputs, arrived)
    output, kept = layer_forward(stream, first, gains, weights, table)

    early = layer_backward(cotangent, kept, first, gains, weights, table, None)
    arrived = lax.ppermute(early.astype(BF16), "section", [(1, 0)]).astype(F32)
    dy = jnp.where(leading, arrived, cotangent)
    grads = Gradients()
    down = layer_backward(dy, kept, first, gains, weights, table, grads)
    found = grads.found
    return (
        output[None],
        down[None],
        found["qkv"],
        found["output"],
        found["gateup"],
        found["down"],
        found["gains"],
    )


def solution(mesh):
    sizes = mesh.shape
    fine = Mesh(
        mesh.devices.reshape(sizes["section"], sizes["shard"], 4, 4, 2),
        ("section", "shard", "z", "x", "core"),
    )
    tokens = ("shard",) + REP
    in_specs = (
        P(tokens, None),
        P(tokens, None),
        P(tokens, None),
        P("section", "shard", None),
        P("section", "shard", None),
        P("section", "shard", None),
        P("section", "shard", None),
        P("section", None, "shard"),
    )
    out_specs = (
        P("section", tokens, None),
        P("section", tokens, None),
        P("section", tokens, None),
        P("section", tokens, None),
        P("section", tokens, None),
        P("section", tokens, None),
        P("section", None, tokens),
    )
    return jax.shard_map(shards, mesh=fine, in_specs=in_specs, out_specs=out_specs, check_vma=False)
```

```python
import functools

import jax
import jax.numpy as jnp
import numpy as np
from jax import lax
from jax.experimental import pallas as pl
from jax.experimental.pallas import tpu as pltpu
from jax.sharding import Mesh
from jax.sharding import PartitionSpec as P

D = 960
HEADS = 15
KV_HEADS = 5
GROUP = HEADS // KV_HEADS
HEAD = 64
FF = 2560
QKV = 1600
ROWS = 112
LANES = 128
BLOCKS = 13
EPSILON = 1e-05
ROPE_BASE = 100000.0
NEGATIVE = -1e30
HEAD_SCALE = HEAD ** (-0.5)
BF16 = jnp.bfloat16
F32 = jnp.float32
REP = ("z", "x", "core")
SWAP = [(0, 1), (1, 0)]
VMEM_LIMIT = 20 * 1024 * 1024


def lane_ids(rows):
    return lax.broadcasted_iota(jnp.int32, (rows, LANES), 1)


def swapped_halves(x, low_half):
    return jnp.where(low_half, pltpu.roll(x, LANES - 32, 1), pltpu.roll(x, 32, 1))


def block_of(ref, index, width):
    start = index * LANES
    stop = min(start + LANES, width)
    part = ref[:, start:stop]
    if stop - start < LANES:
        part = jnp.concatenate([part, jnp.zeros((part.shape[0], LANES - (stop - start)), part.dtype)], axis=1)
    return part


def both_halves(block, slot, left):
    if slot == 0:
        low = jnp.where(left, block, 0.0)
        high = pltpu.roll(low, HEAD, 1)
    else:
        high = jnp.where(left, 0.0, block)
        low = pltpu.roll(high, HEAD, 1)
    return low.astype(BF16), high.astype(BF16)


def contract(a, b, dims):
    return lax.dot_general(a, b, ((dims[0:1], dims[1:2]), ((), ())), preferred_element_type=F32)


def attend_kernel(proj_ref, mask_ref, cos_ref, sin_ref, heads_ref, prob_ref, mixed_ref):
    lanes = lane_ids(ROWS)
    left = lanes < HEAD
    low_half = (lanes % HEAD) < 32
    cos = cos_ref[...]
    sin = sin_ref[...]
    mask = mask_ref[0] > 0.0
    blocks = []
    for b in range(BLOCKS):
        x = block_of(proj_ref, b, QKV)
        if b < 10:
            x = x * cos + swapped_halves(x, low_half) * sin
        low = x.astype(BF16)
        blocks.append(low)
        stop = min(b * LANES + LANES, QKV)
        heads_ref[:, b * LANES : stop] = low[:, : stop - b * LANES]
    mixed = [None] * 8
    for kk in range(KV_HEADS):
        kslot, vslot = HEADS + kk, HEADS + KV_HEADS + kk
        keys = both_halves(blocks[kslot // 2].astype(F32), kslot % 2, left)
        values = both_halves(blocks[vslot // 2].astype(F32), vslot % 2, left)
        for h in range(kk * GROUP, kk * GROUP + GROUP):
            half, b = h % 2, h // 2
            scores = contract(keys[half], blocks[b], (1, 1)) * HEAD_SCALE
            scores = jnp.where(mask, scores, NEGATIVE)
            top = jnp.max(scores, axis=0, keepdims=True)
            raised = jnp.exp(scores - top)
            prob = raised / jnp.sum(raised, axis=0, keepdims=True)
            prob_ref[0, h] = prob
            part = contract(prob.astype(BF16), values[half], (0, 0))
            mixed[b] = part if mixed[b] is None else mixed[b] + part
    for b in range(8):
        stop = min(b * LANES + LANES, D)
        mixed_ref[:, b * LANES : stop] = mixed[b].astype(BF16)[:, : stop - b * LANES]


def attend_back_kernel(heads_ref, prob_ref, dmixed_ref, cos_ref, sin_ref, out_ref):
    lanes = lane_ids(ROWS)
    left = lanes < HEAD
    low_half = (lanes % HEAD) < 32
    cos = cos_ref[...]
    sin = sin_ref[...]
    blocks = [block_of(heads_ref, b, QKV) for b in range(BLOCKS)]
    dmixed = [block_of(dmixed_ref, b, D) for b in range(8)]
    outs = [None] * BLOCKS

    def add(index, term):
        outs[index] = term if outs[index] is None else outs[index] + term

    for kk in range(KV_HEADS):
        kslot, vslot = HEADS + kk, HEADS + KV_HEADS + kk
        keys = both_halves(blocks[kslot // 2].astype(F32), kslot % 2, left)
        values = both_halves(blocks[vslot // 2].astype(F32), vslot % 2, left)
        dkeys = [None, None]
        dvalues = [None, None]
        for h in range(kk * GROUP, kk * GROUP + GROUP):
            half, b = h % 2, h // 2
            prob = prob_ref[0, h]
            dprob = contract(values[half], dmixed[b], (1, 1))
            inner = jnp.sum(dprob * prob, axis=0, keepdims=True)
            dscore = (prob * (dprob - inner)).astype(BF16)
            add(b, contract(dscore, keys[half], (0, 0)))
            dk = contract(dscore, blocks[b], (1, 0))
            dv = contract(prob.astype(BF16), dmixed[b], (1, 0))
            dkeys[half] = dk if dkeys[half] is None else dkeys[half] + dk
            dvalues[half] = dv if dvalues[half] is None else dvalues[half] + dv
        for slot, (low, high) in ((kslot, dkeys), (vslot, dvalues)):
            low = jnp.where(left, low, 0.0)
            high = jnp.where(left, 0.0, high)
            if slot % 2 == 0:
                term = low + pltpu.roll(high, HEAD, 1)
            else:
                term = pltpu.roll(low, HEAD, 1) + high
            add(slot // 2, term)
    for b in range(BLOCKS):
        x = outs[b]
        if b < 10:
            x = x * HEAD_SCALE
            x = x * cos - swapped_halves(x, low_half) * sin
        stop = min(b * LANES + LANES, QKV)
        out_ref[:, b * LANES : stop] = x.astype(BF16)[:, : stop - b * LANES]


def row_spec(width):
    return pl.BlockSpec((ROWS, width), lambda i: (i, 0))


def attend(projected, mask, cos, sin):
    count = mask.shape[0]
    rows = count * ROWS
    return pl.pallas_call(
        attend_kernel,
        grid=(count,),
        in_specs=[
            row_spec(QKV),
            pl.BlockSpec((1, ROWS, ROWS), lambda i: (i, 0, 0)),
            row_spec(LANES),
            row_spec(LANES),
        ],
        out_specs=[
            row_spec(QKV),
            pl.BlockSpec((1, HEADS, ROWS, ROWS), lambda i: (i, 0, 0, 0)),
            row_spec(D),
        ],
        out_shape=[
            jax.ShapeDtypeStruct((rows, QKV), BF16),
            jax.ShapeDtypeStruct((count, HEADS, ROWS, ROWS), F32),
            jax.ShapeDtypeStruct((rows, D), BF16),
        ],
        compiler_params=pltpu.CompilerParams(vmem_limit_bytes=VMEM_LIMIT),
        name="attend",
    )(projected, mask, cos, sin)


def attend_back(heads, prob, dmixed, cos, sin):
    count = prob.shape[0]
    rows = count * ROWS
    return pl.pallas_call(
        attend_back_kernel,
        grid=(count,),
        in_specs=[
            row_spec(QKV),
            pl.BlockSpec((1, HEADS, ROWS, ROWS), lambda i: (i, 0, 0, 0)),
            row_spec(D),
            row_spec(LANES),
            row_spec(LANES),
        ],
        out_specs=row_spec(QKV),
        out_shape=jax.ShapeDtypeStruct((rows, QKV), BF16),
        compiler_params=pltpu.CompilerParams(vmem_limit_bytes=VMEM_LIMIT),
        name="attend_back",
    )(heads, prob, dmixed, cos, sin)


def tables(segments):
    count, rows = segments.shape
    earlier = jnp.sum((segments[:, None, :] < segments[:, :, None]).astype(jnp.int32), axis=2)
    position = (jnp.arange(rows, dtype=jnp.int32)[None, :] - earlier).astype(F32).reshape(count * rows, 1)
    frequency = ROPE_BASE ** (-jnp.arange(HEAD // 2, dtype=F32) * 2.0 / HEAD)
    angles = position * frequency[None, :]
    cos, sin = jnp.cos(angles), jnp.sin(angles)
    order = jnp.arange(rows, dtype=jnp.int32)
    mask = (segments[:, :, None] == segments[:, None, :]) & (order[:, None] <= order[None, :])[None]
    return (
        jnp.concatenate([cos] * 4, axis=1),
        jnp.concatenate([-sin, sin, -sin, sin], axis=1),
        mask.astype(F32),
    )


def mm(a, b):
    return jnp.dot(a, b, preferred_element_type=F32)


def mmt(a, b):
    return lax.dot_general(a, b, (((1,), (1,)), ((), ())), preferred_element_type=F32)


def layer_forward(stream, gains, weights, table):
    qkv_w, out_w, gateup_w, down_w = weights
    cos, sin, mask = table
    first_scale = lax.rsqrt(jnp.mean(stream * stream, axis=-1, keepdims=True) + EPSILON)
    attn_norm = (stream * first_scale * gains[0]).astype(BF16)
    projected = mm(attn_norm, qkv_w)
    heads, prob, mixed = attend(projected, mask, cos, sin)
    middle = stream + mm(mixed, out_w)
    second_scale = lax.rsqrt(jnp.mean(middle * middle, axis=-1, keepdims=True) + EPSILON)
    ffn_norm = (middle * second_scale * gains[1]).astype(BF16)
    gateup = mm(ffn_norm, gateup_w)
    gate, up = gateup[:, :FF], gateup[:, FF:]
    hidden = (gate * jax.nn.sigmoid(gate) * up).astype(BF16)
    output = middle + mm(hidden, down_w)
    return output, (stream, first_scale, attn_norm, heads, prob, mixed, middle, second_scale, ffn_norm, gate, up, hidden)


def norm_back(incoming, gain, scale, normed):
    scaled = incoming * gain
    return scale * (scaled - normed * jnp.mean(scaled * normed, axis=-1, keepdims=True))


def layer_backward(dy, kept, gains, weights, table, grads):
    qkv_w, out_w, gateup_w, down_w = weights
    cos, sin, _ = table
    stream, first_scale, attn_norm, heads, prob, mixed, middle, second_scale, ffn_norm, gate, up, hidden = kept
    dz = dy.astype(BF16)
    if grads is not None:
        dz, _ = lax.optimization_barrier((dz, grads.down(dz)))
    dhidden = mmt(dz, down_w)
    s = jax.nn.sigmoid(gate)
    dgateup = jnp.concatenate(
        [dhidden * up * s * (1.0 + gate * (1.0 - s)), dhidden * gate * s], axis=1
    ).astype(BF16)
    if grads is not None:
        made = grads.gateup(dgateup)
    dffn = mmt(dgateup, gateup_w)
    second_normed = middle * second_scale
    dmiddle = dy + norm_back(dffn, gains[1], second_scale, second_normed)
    dbranch = dmiddle.astype(BF16)
    if grads is not None:
        grads.branch(dbranch)
        dbranch, _ = lax.optimization_barrier((dbranch, made))
    dmixed = mmt(dbranch, out_w).astype(BF16)
    dprojected = attend_back(heads, prob, dmixed, cos, sin)
    dattn = mmt(dprojected, qkv_w)
    first_normed = stream * first_scale
    if grads is not None:
        gain_grads = jnp.stack([jnp.sum(dattn * first_normed, axis=0), jnp.sum(dffn * second_normed, axis=0)], axis=1)
        grads.attention(dprojected, gain_grads)
    return dmiddle + norm_back(dattn, gains[0], first_scale, first_normed)


def place_kernel(plan, count, cut, at_ref, *refs):
    pieces, out_ref, sems = refs[:count], refs[count], refs[count + 1]
    rows = out_ref.shape[1] // cut
    copies = []
    for i, (source, start) in enumerate(plan):
        for j in range(cut):
            copies.append(
                pltpu.make_async_copy(
                    pieces[source].at[pl.ds(start + j * rows, rows)],
                    out_ref.at[at_ref[i], pl.ds(j * rows, rows)],
                    sems.at[i, j],
                )
            )
    for copy in copies:
        copy.start()
    for copy in copies:
        copy.wait()


def placed(pieces, plan, at, depth, width, cut):
    parts = len(plan)
    out = pl.pallas_call(
        functools.partial(place_kernel, plan, len(pieces), cut),
        in_specs=[pl.BlockSpec(memory_space=pltpu.SMEM)] + [pl.BlockSpec(memory_space=pl.ANY)] * len(pieces),
        out_specs=pl.BlockSpec(memory_space=pl.ANY),
        out_shape=jax.ShapeDtypeStruct((parts, depth, width), BF16),
        scratch_shapes=[pltpu.SemaphoreType.DMA((parts, cut))],
        compiler_params=pltpu.CompilerParams(vmem_limit_bytes=VMEM_LIMIT),
        name="placed",
    )(jnp.stack(at).astype(jnp.int32), *pieces)
    return out.reshape(parts * depth, width)


def outer_kernel(l0_ref, r0_ref, l1_ref, r1_ref, out_ref):
    total = contract(l0_ref[...], r0_ref[...], (0, 0)) + contract(l1_ref[...], r1_ref[...], (0, 0))
    out_ref[...] = total.astype(BF16).reshape(out_ref.shape)


def outer(left, right, chunked):
    rows, depth = left[0].shape
    width = right[0].shape[1]
    if chunked:
        tile = depth // 2
        out_spec = pl.BlockSpec((16, 1, tile // 16, width), lambda i: (0, i, 0, 0))
        shape = (16, 2, tile // 16, width)
    else:
        tile = 256
        out_spec = pl.BlockSpec((tile, width), lambda i: (i, 0))
        shape = (depth, width)
    left_spec = pl.BlockSpec((rows, tile), lambda i: (0, i))
    right_spec = pl.BlockSpec((rows, width), lambda i: (0, 0))
    return pl.pallas_call(
        outer_kernel,
        grid=(depth // tile,),
        in_specs=[left_spec, right_spec, left_spec, right_spec],
        out_specs=out_spec,
        out_shape=jax.ShapeDtypeStruct(shape, BF16),
        compiler_params=pltpu.CompilerParams(vmem_limit_bytes=VMEM_LIMIT),
        cost_estimate=pl.CostEstimate(
            flops=4 * rows * depth * width,
            bytes_accessed=2 * depth * width + 4 * rows * (depth + width),
            transcendentals=0,
        ),
        name="outer",
    )(left[0], right[0], left[1], right[1])


def attention_outer_kernel(m0, b0, m1, b1, a0, p0, a1, p1, pick_ref, gain_ref, out_ref):
    first = contract(m0[...], b0[...], (0, 0)) + contract(m1[...], b1[...], (0, 0))
    second = contract(a0[...], p0[...], (0, 0)) + contract(a1[...], p1[...], (0, 0))
    out_ref[:, :1280] = jnp.concatenate([first, second], axis=1).astype(BF16)
    out_ref[:, 1280:] = contract(pick_ref[...], gain_ref[...], (0, 0)).astype(BF16)


def attention_outer(mixed, dbranch, attn, dprojected, pick, gain_grads):
    rows, depth = mixed[0].shape
    tile = 256

    def left(height):
        return pl.BlockSpec((height, tile), lambda i: (0, i))

    def right(height, width):
        return pl.BlockSpec((height, width), lambda i: (0, 0))

    return pl.pallas_call(
        attention_outer_kernel,
        grid=(depth // tile,),
        in_specs=[left(rows), right(rows, 480)] * 2 + [left(rows), right(rows, 800)] * 2
        + [left(D), right(D, LANES)],
        out_specs=pl.BlockSpec((tile, 1280 + LANES), lambda i: (i, 0)),
        out_shape=jax.ShapeDtypeStruct((depth, 1280 + LANES), BF16),
        compiler_params=pltpu.CompilerParams(vmem_limit_bytes=VMEM_LIMIT),
        name="attention_outer",
    )(mixed[0], dbranch[0], mixed[1], dbranch[1], attn[0], dprojected[0], attn[1], dprojected[1], pick, gain_grads)


def ring_scatter(v, axis, dim):
    me = lax.axis_index(axis)
    up = [(i, (i + 1) % 4) for i in range(4)]
    back = [(i, (i + 3) % 4) for i in range(4)]

    def part(step):
        return lax.dynamic_index_in_dim(v, (me + step) % 4, dim, keepdims=False)

    far, following, before = part(2), part(1), part(3)
    cut = far.shape[0] // 2
    from_before = lax.ppermute(far[:cut], axis, up)
    from_after = lax.ppermute(far[cut:], axis, back)
    following = jnp.concatenate([following[:cut] + from_before, following[cut:]], axis=0)
    before = jnp.concatenate([before[:cut], before[cut:] + from_after], axis=0)
    from_before = lax.ppermute(following, axis, up)
    from_after = lax.ppermute(before, axis, back)
    return (part(0).astype(F32) + from_before.astype(F32) + from_after.astype(F32)).astype(BF16)


def row_order():
    pick = np.zeros((D, 1024), np.float32)
    for row in range(D):
        s, rest = divmod(row, 480)
        chunk, i = divmod(rest, 30)
        pick[row, chunk * 64 + s * 32 + i] = 1.0
    return pick


def with_other(x):
    return x, lax.ppermute(x, "core", SWAP)


class Gradients:
    def __init__(self, kept):
        self.core = lax.axis_index("core") == 0
        self.shard = lax.axis_index("shard") == 0
        self.pick = jnp.asarray(row_order(), BF16)
        attn_norm, mixed, ffn_norm, hidden = kept[2], kept[5], kept[8], kept[11]
        self.hidden = with_other(hidden)
        self.ffn = with_other(mm(ffn_norm, self.pick).astype(BF16))
        self.attn = with_other(mm(attn_norm, self.pick).astype(BF16))
        self.mixed = with_other(mm(mixed, self.pick).astype(BF16))

    def shared(self, right):
        cut = right.shape[1] // 2
        keep = jnp.where(self.core, right[:, :cut], right[:, cut:])
        give = jnp.where(self.core, right[:, cut:], right[:, :cut])
        return keep, lax.ppermute(give, "core", SWAP)

    def joined(self, parts):
        shard, core = lax.axis_index("shard"), lax.axis_index("core")
        axes = ("shard", "core")

        def part(s, c):
            return lax.dynamic_index_in_dim(parts, 2 * s + c, 0, keepdims=False)

        across = lax.ppermute(part(1 - shard, core), axes, [(0, 2), (2, 0), (1, 3), (3, 1)]).astype(F32)
        beside = lax.ppermute(part(shard, 1 - core), axes, [(0, 1), (1, 0), (2, 3), (3, 2)]).astype(F32)
        corner = lax.ppermute(part(1 - shard, 1 - core), axes, [(0, 3), (3, 0), (1, 2), (2, 1)]).astype(F32)
        own = part(shard, core).astype(F32) + across
        other = beside + corner
        return jnp.where(self.core, own, other), jnp.where(self.core, other, own)

    def down(self, dz):
        made = outer(self.hidden, self.shared(dz), True).reshape(FF, 480)
        self.down_piece = lax.psum_scatter(made, ("z", "x"), scatter_dimension=0, tiled=True)
        return made

    def gateup(self, dgateup):
        made = outer(self.ffn, self.shared(dgateup), False)
        self.gateup_piece = ring_scatter(ring_scatter(made.reshape(4, 4, 64, FF), "x", 1), "z", 0)
        return made

    def branch(self, dbranch):
        self.dbranch = self.shared(dbranch)

    def attention(self, dprojected, gain_grads):
        gain_grads = jnp.pad(gain_grads.astype(BF16), ((0, 0), (0, LANES - 2)))
        made = attention_outer(self.mixed, self.dbranch, self.attn, self.shared(dprojected), self.pick, gain_grads)
        width = made.shape[1]
        self.attention_piece = ring_scatter(ring_scatter(made.reshape(4, 4, 64, width), "z", 0), "x", 0)

    def finish(self):
        def by_owner(piece):
            piece = piece.reshape(2, 32, piece.shape[1])
            both = jnp.stack([piece[:, :16], piece[:, 15:31]], axis=1)
            return both.reshape(4, 16, piece.shape[2])

        tail = jnp.pad(self.down_piece.reshape(4, 40, 480), ((0, 0), (0, 8), (0, 32)))
        parts = jnp.concatenate(
            [by_owner(self.gateup_piece), by_owner(self.attention_piece)]
            + [tail[:, 16 * i : 16 * i + 16] for i in range(3)],
            axis=2,
        )
        low, high = self.joined(parts)

        def columns(start, width, rows):
            return jnp.concatenate(
                [low[:rows, start : start + width], high[:rows, start : start + width]], axis=1
            )

        gateup = columns(0, FF, 15)
        output = columns(FF, 480, 15)
        qkv = columns(FF + 480, 800, 15)
        at = FF + 1280
        gains = (low[:15, at : at + 2] + high[:15, at : at + 2]).T
        at += LANES
        down = jnp.concatenate([columns(at, 480, 16), columns(at + 512, 480, 16), columns(at + 1024, 480, 8)], axis=0)
        return qkv[None], output[None], gateup[None], down[None], gains[None]


def shards(tokens, segments, cotangent, qkv_weight, output_weight, gateup_weight, down_weight, norm_gains):
    leading = lax.axis_index("section") == 0
    first = lax.axis_index("shard") == 0
    rep = lax.axis_index(REP)

    core = lax.axis_index("core")
    shard = lax.axis_index("shard")
    rows = lax.dynamic_slice_in_dim(gateup_weight[0], jnp.minimum(rep * 16, 464), 16, 0)
    gateup_other = lax.all_gather(lax.ppermute(rows, "shard", SWAP), REP, axis=0, tiled=True)
    own_gains = norm_gains[0]
    other_gains = lax.ppermute(own_gains, "shard", SWAP)
    gains = jnp.concatenate(
        [jnp.where(first, own_gains, other_gains), jnp.where(first, other_gains, own_gains)], axis=1
    ).astype(F32)

    def whole(own):
        depth, width = own.shape
        half = depth // 2
        got = lax.ppermute(lax.dynamic_slice_in_dim(own, core * half, half, 0), "shard", SWAP)
        beside = lax.ppermute(got, "core", SWAP)
        place = 2 * (1 - shard)
        return placed(
            (own, got, beside),
            ((0, 0), (0, half), (1, 0), (2, 0)),
            (2 * shard, 2 * shard + 1, place + core, place + 1 - core),
            half, width, 2 if half == 640 else 1,
        )

    weights = (
        whole(qkv_weight[0]),
        whole(output_weight[0]),
        placed((gateup_weight[0], gateup_other), ((0, 0), (1, 0)), (shard, 1 - shard), 480, 2 * FF, 6),
        whole(down_weight[0]),
    )

    table = tables(segments)
    inputs = tokens.astype(F32)
    early, _ = layer_forward(inputs, gains, weights, table)
    arrived = lax.ppermute(early.astype(BF16), "section", [(0, 1)]).astype(F32)
    stream = jnp.where(leading, inputs, arrived)
    output, kept = layer_forward(stream, gains, weights, table)

    grads = Gradients(kept)
    early = layer_backward(cotangent, kept, gains, weights, table, None)
    arrived = lax.ppermute(early.astype(BF16), "section", [(1, 0)]).astype(F32)
    dy = jnp.where(leading, arrived, cotangent)
    down = layer_backward(dy, kept, gains, weights, table, grads)
    return (output[None], down[None], *grads.finish())


def solution(mesh):
    sizes = mesh.shape
    fine = Mesh(
        mesh.devices.reshape(sizes["section"], sizes["shard"], 4, 4, 2),
        ("section", "shard", "z", "x", "core"),
    )
    tokens = ("shard",) + REP
    in_specs = (
        P(tokens, None),
        P(tokens, None),
        P(tokens, None),
        P("section", "shard", None),
        P("section", "shard", None),
        P("section", "shard", None),
        P("section", "shard", None),
        P("section", None, "shard"),
    )
    out_specs = (
        P("section", tokens, None),
        P("section", tokens, None),
        P("section", tokens, None),
        P("section", tokens, None),
        P("section", tokens, None),
        P("section", tokens, None),
        P("section", None, tokens),
    )
    return jax.shard_map(shards, mesh=fine, in_specs=in_specs, out_specs=out_specs, check_vma=False)
```

```python
import functools

import jax
import jax.numpy as jnp
import numpy as np
from jax import lax
from jax.experimental import pallas as pl
from jax.experimental.pallas import tpu as pltpu
from jax.sharding import Mesh
from jax.sharding import PartitionSpec as P

D = 960
HEADS = 15
KV_HEADS = 5
GROUP = HEADS // KV_HEADS
HEAD = 64
FF = 2560
QKV = 1600
ROWS = 112
LANES = 128
BLOCKS = 13
EPSILON = 1e-05
ROPE_BASE = 100000.0
NEGATIVE = -1e30
HEAD_SCALE = HEAD ** (-0.5)
BF16 = jnp.bfloat16
F32 = jnp.float32
REP = ("z", "x", "core")
SWAP = [(0, 1), (1, 0)]
VMEM_LIMIT = 12 * 1024 * 1024
OUTER_LIMIT = 20 * 1024 * 1024


def lane_ids(rows):
    return lax.broadcasted_iota(jnp.int32, (rows, LANES), 1)


def swapped_halves(x, low_half):
    return jnp.where(low_half, pltpu.roll(x, LANES - 32, 1), pltpu.roll(x, 32, 1))


def block_of(ref, index, width):
    start = index * LANES
    stop = min(start + LANES, width)
    part = ref[:, start:stop]
    if stop - start < LANES:
        part = jnp.concatenate([part, jnp.zeros((part.shape[0], LANES - (stop - start)), part.dtype)], axis=1)
    return part


def both_halves(block, slot, left):
    if slot == 0:
        low = jnp.where(left, block, 0.0)
        high = pltpu.roll(low, HEAD, 1)
    else:
        high = jnp.where(left, 0.0, block)
        low = pltpu.roll(high, HEAD, 1)
    return low.astype(BF16), high.astype(BF16)


def contract(a, b, dims):
    return lax.dot_general(a, b, ((dims[0:1], dims[1:2]), ((), ())), preferred_element_type=F32)


def attend_kernel(proj_ref, mask_ref, cos_ref, sin_ref, heads_ref, prob_ref, mixed_ref):
    lanes = lane_ids(ROWS)
    left = lanes < HEAD
    low_half = (lanes % HEAD) < 32
    cos = cos_ref[...]
    sin = sin_ref[...]
    mask = mask_ref[0] > 0.0
    blocks = []
    for b in range(BLOCKS):
        x = block_of(proj_ref, b, QKV)
        if b < 10:
            x = x * cos + swapped_halves(x, low_half) * sin
        low = x.astype(BF16)
        blocks.append(low)
        stop = min(b * LANES + LANES, QKV)
        heads_ref[:, b * LANES : stop] = low[:, : stop - b * LANES]
    mixed = [None] * 8
    for kk in range(KV_HEADS):
        kslot, vslot = HEADS + kk, HEADS + KV_HEADS + kk
        keys = both_halves(blocks[kslot // 2].astype(F32), kslot % 2, left)
        values = both_halves(blocks[vslot // 2].astype(F32), vslot % 2, left)
        for h in range(kk * GROUP, kk * GROUP + GROUP):
            half, b = h % 2, h // 2
            scores = contract(keys[half], blocks[b], (1, 1)) * HEAD_SCALE
            scores = jnp.where(mask, scores, NEGATIVE)
            top = jnp.max(scores, axis=0, keepdims=True)
            raised = jnp.exp(scores - top)
            prob = raised / jnp.sum(raised, axis=0, keepdims=True)
            prob_ref[0, h] = prob
            part = contract(prob.astype(BF16), values[half], (0, 0))
            mixed[b] = part if mixed[b] is None else mixed[b] + part
    for b in range(8):
        stop = min(b * LANES + LANES, D)
        mixed_ref[:, b * LANES : stop] = mixed[b].astype(BF16)[:, : stop - b * LANES]


def attend_back_kernel(heads_ref, prob_ref, dmixed_ref, cos_ref, sin_ref, out_ref):
    lanes = lane_ids(ROWS)
    left = lanes < HEAD
    low_half = (lanes % HEAD) < 32
    cos = cos_ref[...]
    sin = sin_ref[...]
    blocks = [block_of(heads_ref, b, QKV) for b in range(BLOCKS)]
    dmixed = [block_of(dmixed_ref, b, D) for b in range(8)]
    outs = [None] * BLOCKS

    def add(index, term):
        outs[index] = term if outs[index] is None else outs[index] + term

    for kk in range(KV_HEADS):
        kslot, vslot = HEADS + kk, HEADS + KV_HEADS + kk
        keys = both_halves(blocks[kslot // 2].astype(F32), kslot % 2, left)
        values = both_halves(blocks[vslot // 2].astype(F32), vslot % 2, left)
        dkeys = [None, None]
        dvalues = [None, None]
        for h in range(kk * GROUP, kk * GROUP + GROUP):
            half, b = h % 2, h // 2
            prob = prob_ref[0, h]
            dprob = contract(values[half], dmixed[b], (1, 1))
            inner = jnp.sum(dprob * prob, axis=0, keepdims=True)
            dscore = (prob * (dprob - inner)).astype(BF16)
            add(b, contract(dscore, keys[half], (0, 0)))
            dk = contract(dscore, blocks[b], (1, 0))
            dv = contract(prob.astype(BF16), dmixed[b], (1, 0))
            dkeys[half] = dk if dkeys[half] is None else dkeys[half] + dk
            dvalues[half] = dv if dvalues[half] is None else dvalues[half] + dv
        for slot, (low, high) in ((kslot, dkeys), (vslot, dvalues)):
            low = jnp.where(left, low, 0.0)
            high = jnp.where(left, 0.0, high)
            if slot % 2 == 0:
                term = low + pltpu.roll(high, HEAD, 1)
            else:
                term = pltpu.roll(low, HEAD, 1) + high
            add(slot // 2, term)
    for b in range(BLOCKS):
        x = outs[b]
        if b < 10:
            x = x * HEAD_SCALE
            x = x * cos - swapped_halves(x, low_half) * sin
        stop = min(b * LANES + LANES, QKV)
        out_ref[:, b * LANES : stop] = x.astype(BF16)[:, : stop - b * LANES]


def row_spec(width):
    return pl.BlockSpec((ROWS, width), lambda i: (i, 0))


def attend(projected, mask, cos, sin):
    count = mask.shape[0]
    rows = count * ROWS
    return pl.pallas_call(
        attend_kernel,
        grid=(count,),
        in_specs=[
            row_spec(QKV),
            pl.BlockSpec((1, ROWS, ROWS), lambda i: (i, 0, 0)),
            row_spec(LANES),
            row_spec(LANES),
        ],
        out_specs=[
            row_spec(QKV),
            pl.BlockSpec((1, HEADS, ROWS, ROWS), lambda i: (i, 0, 0, 0)),
            row_spec(D),
        ],
        out_shape=[
            jax.ShapeDtypeStruct((rows, QKV), BF16),
            jax.ShapeDtypeStruct((count, HEADS, ROWS, ROWS), F32),
            jax.ShapeDtypeStruct((rows, D), BF16),
        ],
        compiler_params=pltpu.CompilerParams(vmem_limit_bytes=VMEM_LIMIT),
        name="attend",
    )(projected, mask, cos, sin)


def attend_back(heads, prob, dmixed, cos, sin):
    count = prob.shape[0]
    rows = count * ROWS
    return pl.pallas_call(
        attend_back_kernel,
        grid=(count,),
        in_specs=[
            row_spec(QKV),
            pl.BlockSpec((1, HEADS, ROWS, ROWS), lambda i: (i, 0, 0, 0)),
            row_spec(D),
            row_spec(LANES),
            row_spec(LANES),
        ],
        out_specs=row_spec(QKV),
        out_shape=jax.ShapeDtypeStruct((rows, QKV), BF16),
        compiler_params=pltpu.CompilerParams(vmem_limit_bytes=VMEM_LIMIT),
        name="attend_back",
    )(heads, prob, dmixed, cos, sin)


def tables(segments):
    count, rows = segments.shape
    earlier = jnp.sum((segments[:, None, :] < segments[:, :, None]).astype(jnp.int32), axis=2)
    position = (jnp.arange(rows, dtype=jnp.int32)[None, :] - earlier).astype(F32).reshape(count * rows, 1)
    frequency = ROPE_BASE ** (-jnp.arange(HEAD // 2, dtype=F32) * 2.0 / HEAD)
    angles = position * frequency[None, :]
    cos, sin = jnp.cos(angles), jnp.sin(angles)
    order = jnp.arange(rows, dtype=jnp.int32)
    mask = (segments[:, :, None] == segments[:, None, :]) & (order[:, None] <= order[None, :])[None]
    return (
        jnp.concatenate([cos] * 4, axis=1),
        jnp.concatenate([-sin, sin, -sin, sin], axis=1),
        mask.astype(F32),
    )


def mm(a, b):
    return jnp.dot(a, b, preferred_element_type=F32)


def mmt(a, b):
    return lax.dot_general(a, b, (((1,), (1,)), ((), ())), preferred_element_type=F32)


def layer_forward(stream, gains, weights, table, mm_out=mm, mm_gateup=mm, then=lambda mixed: mixed):
    cos, sin, mask = table
    first_scale = lax.rsqrt(jnp.mean(stream * stream, axis=-1, keepdims=True) + EPSILON)
    attn_norm = (stream * first_scale * gains[0]).astype(BF16)
    projected = mm(attn_norm, weights[0])
    heads, prob, mixed = attend(projected, mask, cos, sin)
    mixed = then(mixed)
    middle = stream + mm_out(mixed, weights[1])
    second_scale = lax.rsqrt(jnp.mean(middle * middle, axis=-1, keepdims=True) + EPSILON)
    ffn_norm = (middle * second_scale * gains[1]).astype(BF16)
    gateup = mm_gateup(ffn_norm, weights[2])
    gate, up = gateup[:, :FF], gateup[:, FF:]
    hidden = (gate * jax.nn.sigmoid(gate) * up).astype(BF16)
    output = middle + mmt(hidden, weights[3])
    return output, (stream, first_scale, attn_norm, heads, prob, mixed, middle, second_scale, ffn_norm, gate, up, hidden)


def norm_back(incoming, gain, scale, normed):
    scaled = incoming * gain
    return scale * (scaled - normed * jnp.mean(scaled * normed, axis=-1, keepdims=True))


def layer_backward(dy, kept, gains, weights, table, grads):
    qkv_w, out_w, gateup_w, down_w = weights
    cos, sin, _ = table
    stream, first_scale, attn_norm, heads, prob, mixed, middle, second_scale, ffn_norm, gate, up, hidden = kept
    dz = dy.astype(BF16)
    dhidden = mm(dz, down_w)
    s = jax.nn.sigmoid(gate)
    dgateup = jnp.concatenate(
        [dhidden * up * s * (1.0 + gate * (1.0 - s)), dhidden * gate * s], axis=1
    ).astype(BF16)
    if grads is not None:
        made = grads.gateup(dgateup)
    dffn = mmt(dgateup, gateup_w)
    second_normed = middle * second_scale
    dmiddle = dy + norm_back(dffn, gains[1], second_scale, second_normed)
    dbranch = dmiddle.astype(BF16)
    if grads is not None:
        grads.branch(dbranch)
        dbranch, dz, _ = lax.optimization_barrier((dbranch, dz, made))
        dbranch, _ = lax.optimization_barrier((dbranch, grads.down(dz)))
    dmixed = mmt(dbranch, out_w).astype(BF16)
    dprojected = attend_back(heads, prob, dmixed, cos, sin)
    if grads is not None:
        dprojected = grads.heads(dprojected)
    dattn = mmt(dprojected, qkv_w)
    first_normed = stream * first_scale
    if grads is not None:
        gain_grads = jnp.stack([jnp.sum(dattn * first_normed, axis=0), jnp.sum(dffn * second_normed, axis=0)])
        grads.attention(gain_grads)
    return dmiddle + norm_back(dattn, gains[0], first_scale, first_normed)


def place_kernel(counts, at_ref, *refs):
    out_ref = refs[-1]
    step = pl.program_id(0)
    first = 0
    for ref, count in zip(refs, counts):

        @pl.when((step >= first) & (step < first + count))
        def _(ref=ref):
            out_ref[...] = ref[...]

        first += count


def placed(pieces, counts, at, block, shape, base=None):
    firsts = np.cumsum([0] + list(counts))
    bases = () if base is None else (base,)

    def piece_spec(p):
        start, count = int(firsts[p]), counts[p]
        return pl.BlockSpec(block, lambda i, at_ref: (jnp.clip(i - start, 0, count - 1), 0))

    return pl.pallas_call(
        functools.partial(place_kernel, counts),
        grid_spec=pltpu.PrefetchScalarGridSpec(
            num_scalar_prefetch=1,
            grid=(int(firsts[-1]),),
            in_specs=[piece_spec(p) for p in range(len(pieces))] + [pl.BlockSpec(memory_space=pl.ANY)] * len(bases),
            out_specs=pl.BlockSpec(block, lambda i, at_ref: (at_ref[0, i], at_ref[1, i])),
        ),
        out_shape=jax.ShapeDtypeStruct(shape, BF16),
        compiler_params=pltpu.CompilerParams(vmem_limit_bytes=VMEM_LIMIT),
        input_output_aliases={1 + len(pieces): 0} if bases else {},
        name="placed",
    )(jnp.stack(at).astype(jnp.int32), *pieces, *bases)


def outer_kernel(l0_ref, r0_ref, l1_ref, r1_ref, out_ref):
    total = contract(l0_ref[...], r0_ref[...], (0, 0)) + contract(l1_ref[...], r1_ref[...], (0, 0))
    out_ref[...] = total.astype(BF16).reshape(out_ref.shape)


def outer(left, right, chunked):
    rows, depth = left[0].shape
    width = right[0].shape[1]
    if chunked:
        tile = depth // 2
        out_spec = pl.BlockSpec((16, 1, tile // 16, width), lambda i: (0, i, 0, 0))
        shape = (16, 2, tile // 16, width)
    else:
        tile = 256
        out_spec = pl.BlockSpec((tile, width), lambda i: (i, 0))
        shape = (depth, width)
    left_spec = pl.BlockSpec((rows, tile), lambda i: (0, i))
    right_spec = pl.BlockSpec((rows, width), lambda i: (0, 0))
    return pl.pallas_call(
        outer_kernel,
        grid=(depth // tile,),
        in_specs=[left_spec, right_spec, left_spec, right_spec],
        out_specs=out_spec,
        out_shape=jax.ShapeDtypeStruct(shape, BF16),
        compiler_params=pltpu.CompilerParams(vmem_limit_bytes=OUTER_LIMIT),
        cost_estimate=pl.CostEstimate(
            flops=4 * rows * depth * width,
            bytes_accessed=2 * depth * width + 4 * rows * (depth + width),
            transcendentals=0,
        ),
        name="outer",
    )(left[0], right[0], left[1], right[1])


def attention_outer_kernel(m0, b0, m1, b1, a0, p0, a1, p1, pick_ref, gain_ref, out_ref):
    first = contract(m0[...], b0[...], (0, 0)) + contract(m1[...], b1[...], (0, 0))
    second = contract(a0[...], p0[...], (0, 0)) + contract(a1[...], p1[...], (0, 0))
    out_ref[:, :1280] = jnp.concatenate([first, second], axis=1).astype(BF16)
    out_ref[:, 1280:] = contract(pick_ref[...], gain_ref[...], (0, 1)).astype(BF16)


def attention_outer(mixed, dbranch, attn, dprojected, pick, gain_grads):
    rows, depth = mixed[0].shape
    tile = 256

    def left(height):
        return pl.BlockSpec((height, tile), lambda i: (0, i))

    def right(height, width):
        return pl.BlockSpec((height, width), lambda i: (0, 0))

    return pl.pallas_call(
        attention_outer_kernel,
        grid=(depth // tile,),
        in_specs=[left(rows), right(rows, 480)] * 2 + [left(rows), right(rows, 800)] * 2
        + [left(D), right(LANES, D)],
        out_specs=pl.BlockSpec((tile, 1280 + LANES), lambda i: (i, 0)),
        out_shape=jax.ShapeDtypeStruct((depth, 1280 + LANES), BF16),
        compiler_params=pltpu.CompilerParams(vmem_limit_bytes=OUTER_LIMIT),
        name="attention_outer",
    )(mixed[0], dbranch[0], mixed[1], dbranch[1], attn[0], dprojected[0], attn[1], dprojected[1], pick, gain_grads)


class Ring:
    def __init__(self, v, axis, dim):
        self.v, self.axis, self.dim = v, axis, dim
        self.me = lax.axis_index(axis)
        far, after, ahead = self.part(2), self.part(1), self.part(3)
        cut = self.cut = far.shape[0] // 2
        self.low = self.up(jnp.concatenate([far[:cut], after[cut:]], axis=0))
        self.high = self.back(jnp.concatenate([far[cut:], ahead[:cut]], axis=0))

    def up(self, x):
        return lax.ppermute(x, self.axis, [(i, (i + 1) % 4) for i in range(4)])

    def back(self, x):
        return lax.ppermute(x, self.axis, [(i, (i + 3) % 4) for i in range(4)])

    def part(self, step):
        return lax.dynamic_index_in_dim(self.v, (self.me + step) % 4, self.dim, keepdims=False)

    def arrive(self, dep):
        self.low, self.high, dep = lax.optimization_barrier((self.low, self.high, dep))
        return dep

    def passed(self):
        cut = self.cut
        return self.part(1)[:cut] + self.low[:cut], self.part(3)[cut:] + self.high[:cut]

    def second(self, passed):
        self.low_end, self.high_end = self.up(passed[0]), self.back(passed[1])

    def last(self):
        cut, own = self.cut, self.part(0).astype(F32)
        low = own[:cut] + self.low_end.astype(F32) + self.high[cut:].astype(F32)
        high = own[cut:] + self.high_end.astype(F32) + self.low[cut:].astype(F32)
        return jnp.concatenate([low, high], axis=0).astype(BF16)


def meet(one, step, two, end):
    names = {"arrive": ("low", "high"), "end": ("low_end", "high_end")}
    pairs = [(one, n) for n in names[step]] + [(two, n) for n in names[end]]
    for (ring, n), value in zip(pairs, lax.optimization_barrier(tuple(getattr(r, n) for r, n in pairs))):
        setattr(ring, n, value)


def row_order():
    pick = np.zeros((D, 1024), np.float32)
    for row in range(D):
        s, rest = divmod(row, 480)
        chunk, i = divmod(rest, 30)
        pick[row, chunk * 64 + s * 32 + i] = 1.0
    return pick


def with_other(x):
    return x, lax.ppermute(x, "core", SWAP)


class Gradients:
    def __init__(self, kept):
        self.core = lax.axis_index("core") == 0
        self.shard = lax.axis_index("shard") == 0
        self.pick = jnp.asarray(row_order(), BF16)
        attn_norm, mixed, ffn_norm, hidden = kept[2], kept[5], kept[8], kept[11]
        self.hidden = with_other(hidden)
        self.ffn = with_other(mm(ffn_norm, self.pick).astype(BF16))
        self.attn = with_other(mm(attn_norm, self.pick).astype(BF16))
        self.mixed = with_other(mm(mixed, self.pick).astype(BF16))

    def ready(self, dep):
        lefts = (self.hidden, self.ffn, self.attn, self.mixed)
        lefts, dep = lax.optimization_barrier((lefts, dep))
        self.hidden, self.ffn, self.attn, self.mixed = lefts
        return dep

    def shared(self, right):
        cut = right.shape[1] // 2
        keep = jnp.where(self.core, right[:, :cut], right[:, cut:])
        give = jnp.where(self.core, right[:, cut:], right[:, :cut])
        return keep, lax.ppermute(give, "core", SWAP)

    def joined(self, parts):
        shard, core = lax.axis_index("shard"), lax.axis_index("core")
        axes = ("shard", "core")

        def part(s, c):
            return lax.dynamic_index_in_dim(parts, 2 * s + c, 0, keepdims=False)

        across = lax.ppermute(part(1 - shard, core), axes, [(0, 2), (2, 0), (1, 3), (3, 1)]).astype(F32)
        beside = lax.ppermute(part(shard, 1 - core), axes, [(0, 1), (1, 0), (2, 3), (3, 2)]).astype(F32)
        corner = lax.ppermute(part(1 - shard, 1 - core), axes, [(0, 3), (3, 0), (1, 2), (2, 1)]).astype(F32)
        own = part(shard, core).astype(F32) + across
        other = beside + corner
        return jnp.where(self.core, own, other), jnp.where(self.core, other, own)

    def down(self, dz):
        made = outer(self.hidden, self.shared(dz), True)
        self.down_ring = Ring(made.reshape(4, 4, 160, 480), "x", 1)
        return made

    def gateup(self, dgateup):
        made = outer(self.ffn, self.shared(dgateup), False)
        self.gateup_piece = lax.psum_scatter(made, ("z", "x"), scatter_dimension=0, tiled=True)
        return made

    def branch(self, dbranch):
        self.dbranch = self.shared(dbranch)

    def heads(self, dprojected):
        self.dprojected = self.shared(dprojected)
        return dprojected

    def attention(self, gain_grads):
        gain_grads = jnp.pad(gain_grads.astype(BF16), ((0, LANES - 2), (0, 0)))
        made = attention_outer(self.mixed, self.dbranch, self.attn, self.dprojected, self.pick, gain_grads)
        width = made.shape[1]
        down = self.down_ring
        made = down.arrive(made)
        attention = Ring(made.reshape(4, 4, 64, width), "z", 0)
        down.second(down.passed())
        meet(attention, "arrive", down, "end")
        attention.second(attention.passed())
        down = Ring(down.last(), "z", 0)
        meet(down, "arrive", attention, "end")
        self.gateup_piece, attention.low_end = lax.optimization_barrier((self.gateup_piece, attention.low_end))
        attention = Ring(attention.last(), "x", 0)
        down.second(down.passed())
        meet(attention, "arrive", down, "end")
        attention.second(attention.passed())
        self.down_piece, self.attention_piece = down.last(), attention.last()

    def finish(self):
        def by_owner(piece):
            piece = piece.reshape(2, 32, piece.shape[1])
            both = jnp.stack([piece[:, :16], piece[:, 15:31]], axis=1)
            return both.reshape(4, 16, piece.shape[2])

        def columns(pair, start, width):
            return jnp.concatenate([half[:15, start : start + width] for half in pair], axis=1)[None]

        down = jnp.concatenate(self.joined(self.down_piece.reshape(4, 40, 480)), axis=1)[None]
        pair = self.joined(by_owner(self.attention_piece))
        output, qkv = columns(pair, 0, 480), columns(pair, 480, 800)
        gains = (pair[0][:15, 1280:1282] + pair[1][:15, 1280:1282]).T[None]
        gateup = columns(self.joined(by_owner(self.gateup_piece)), 0, FF)
        return qkv, output, gateup, down, gains


def shards(tokens, segments, cotangent, qkv_weight, output_weight, gateup_weight, down_weight, norm_gains):
    leading = lax.axis_index("section") == 0
    first = lax.axis_index("shard") == 0
    rep = lax.axis_index(REP)

    core = lax.axis_index("core")
    shard = lax.axis_index("shard")
    own_out, own_gateup = output_weight[0], gateup_weight[0]
    rows = jnp.concatenate(
        [lax.dynamic_slice_in_dim(w, jnp.minimum(rep * 16, 464), 16, 0) for w in (own_gateup, own_out)], axis=1
    )
    others = lax.all_gather(lax.ppermute(rows, "shard", SWAP), REP, axis=0, tiled=True)
    own_gains = norm_gains[0]
    other_gains = lax.ppermute(own_gains, "shard", SWAP)
    gains = jnp.concatenate(
        [jnp.where(first, own_gains, other_gains), jnp.where(first, other_gains, own_gains)], axis=1
    ).astype(F32)

    def sent(own):
        half = own.shape[0] // 2
        return lax.ppermute(lax.dynamic_slice_in_dim(own, core * half, half, 0), "shard", SWAP)

    def whole(own, got):
        half, width = got.shape
        beside = lax.ppermute(got, "core", SWAP)
        place = 2 * (1 - shard)
        at = jnp.stack([2 * shard, 2 * shard + 1, place + core, place + 1 - core])
        return placed((own, got, beside), (2, 1, 1), (at, at * 0), (half, width), (4 * half, width))

    def own_turned(own):
        depth, width = own.shape
        rows = jnp.arange(4)
        return placed((own,), (4,), (rows, rows * 0 + shard), (depth // 4, width), (depth, 2 * width))

    def whole_turned(base, got):
        half, width = got.shape
        beside = lax.ppermute(got, "core", SWAP)
        rows = jnp.stack([2 * core, 2 * core + 1, 2 - 2 * core, 3 - 2 * core])
        return placed((got, beside), (2, 2), (rows, rows * 0 + 1 - shard), (half // 2, width), base.shape, base)

    def own_first(own, rows):
        at = shard * (480 // rows) + jnp.arange(480 // rows)
        return placed((own,), (480 // rows,), (at, at * 0), (rows, own.shape[1]), (D, own.shape[1]))

    def beside_own(base, other, rows):
        at = (1 - shard) * (480 // rows) + jnp.arange(480 // rows)
        return placed((other,), (480 // rows,), (at, at * 0), (rows, base.shape[1]), base.shape, base)

    def halved(x, pieces):
        cut = D // 2
        own = jnp.where(first, x[:, :cut], x[:, cut:])
        other = jnp.pad(jnp.where(first, x[:, cut:], x[:, :cut]), ((0, 0), (0, 32)))
        return mm(own, pieces[0]) + mm(other, pieces[1])

    turned = down_weight[0].T
    coming = [sent(qkv_weight[0]), sent(turned)]
    qkv_w = whole(qkv_weight[0], coming[0])

    table = tables(segments)
    inputs = tokens.astype(F32)
    down_base, out_base, gateup_base = own_turned(turned), own_first(own_out, 240), own_first(own_gateup, 80)
    parts = [qkv_w, (own_out, others[:, 2 * FF :]), (own_gateup, others[:, : 2 * FF]), None]

    def fetch_down(mixed):
        mixed, got = lax.optimization_barrier((mixed, coming[1]))
        parts[3] = whole_turned(down_base, got)
        return mixed

    early, _ = layer_forward(inputs, gains, parts, table, halved, halved, fetch_down)
    early = early.astype(BF16)
    arrived = lax.ppermute(early, "section", [(0, 1)])
    _, others = lax.optimization_barrier((early, others))
    weights = (qkv_w, beside_own(out_base, others[:, 2 * FF :], 240), beside_own(gateup_base, others, 80), parts[3])
    arrived, weights = lax.optimization_barrier((arrived, weights))
    arrived = arrived.astype(F32)
    stream = jnp.where(leading, inputs, arrived)
    output, kept = layer_forward(stream, gains, weights, table)

    early = layer_backward(cotangent, kept, gains, weights, table, None).astype(BF16)
    arrived = lax.ppermute(early, "section", [(1, 0)])
    _, kept = lax.optimization_barrier((early, kept))
    grads = Gradients(kept)
    arrived = grads.ready(arrived).astype(F32)
    dy = lax.optimization_barrier(jnp.where(leading, arrived, cotangent))
    down = layer_backward(dy, kept, gains, weights, table, grads)
    return (output[None], down[None], *grads.finish())


def solution(mesh):
    sizes = mesh.shape
    fine = Mesh(
        mesh.devices.reshape(sizes["section"], sizes["shard"], 4, 4, 2),
        ("section", "shard", "z", "x", "core"),
    )
    tokens = ("shard",) + REP
    in_specs = (
        P(tokens, None),
        P(tokens, None),
        P(tokens, None),
        P("section", "shard", None),
        P("section", "shard", None),
        P("section", "shard", None),
        P("section", "shard", None),
        P("section", None, "shard"),
    )
    out_specs = (
        P("section", tokens, None),
        P("section", tokens, None),
        P("section", tokens, None),
        P("section", tokens, None),
        P("section", tokens, None),
        P("section", tokens, None),
        P("section", None, tokens),
    )
    return jax.shard_map(shards, mesh=fine, in_specs=in_specs, out_specs=out_specs, check_vma=False)
```

```python
import functools

import jax
import jax.numpy as jnp
import numpy as np
from jax import lax
from jax.experimental import pallas as pl
from jax.experimental.pallas import tpu as pltpu
from jax.sharding import Mesh
from jax.sharding import PartitionSpec as P

D = 960
HEADS = 15
KV_HEADS = 5
GROUP = HEADS // KV_HEADS
HEAD = 64
FF = 2560
QKV = 1600
ROWS = 112
LANES = 128
BLOCKS = 13
EPSILON = 1e-05
ROPE_BASE = 100000.0
NEGATIVE = -1e30
HEAD_SCALE = HEAD ** (-0.5)
BF16 = jnp.bfloat16
F32 = jnp.float32
REP = ("z", "x", "core")
SWAP = [(0, 1), (1, 0)]
VMEM_LIMIT = 12 * 1024 * 1024
OUTER_LIMIT = 20 * 1024 * 1024


def lane_ids(rows):
    return lax.broadcasted_iota(jnp.int32, (rows, LANES), 1)


def swapped_halves(x, low_half):
    return jnp.where(low_half, pltpu.roll(x, LANES - 32, 1), pltpu.roll(x, 32, 1))


def block_of(ref, index, width):
    start = index * LANES
    stop = min(start + LANES, width)
    part = ref[:, start:stop]
    if stop - start < LANES:
        part = jnp.concatenate([part, jnp.zeros((part.shape[0], LANES - (stop - start)), part.dtype)], axis=1)
    return part


def both_halves(block, slot, left):
    if slot == 0:
        low = jnp.where(left, block, 0.0)
        high = pltpu.roll(low, HEAD, 1)
    else:
        high = jnp.where(left, 0.0, block)
        low = pltpu.roll(high, HEAD, 1)
    return low.astype(BF16), high.astype(BF16)


def contract(a, b, dims):
    return lax.dot_general(a, b, ((dims[0:1], dims[1:2]), ((), ())), preferred_element_type=F32)


def attend_kernel(proj_ref, mask_ref, cos_ref, sin_ref, heads_ref, prob_ref, mixed_ref):
    lanes = lane_ids(ROWS)
    left = lanes < HEAD
    low_half = (lanes % HEAD) < 32
    cos = cos_ref[...]
    sin = sin_ref[...]
    mask = mask_ref[0] > 0.0
    blocks = []
    for b in range(BLOCKS):
        x = block_of(proj_ref, b, QKV)
        if b < 10:
            x = x * cos + swapped_halves(x, low_half) * sin
        low = x.astype(BF16)
        blocks.append(low)
        stop = min(b * LANES + LANES, QKV)
        heads_ref[:, b * LANES : stop] = low[:, : stop - b * LANES]
    mixed = [None] * 8
    for kk in range(KV_HEADS):
        kslot, vslot = HEADS + kk, HEADS + KV_HEADS + kk
        keys = both_halves(blocks[kslot // 2].astype(F32), kslot % 2, left)
        values = both_halves(blocks[vslot // 2].astype(F32), vslot % 2, left)
        for h in range(kk * GROUP, kk * GROUP + GROUP):
            half, b = h % 2, h // 2
            scores = contract(keys[half], blocks[b], (1, 1)) * HEAD_SCALE
            scores = jnp.where(mask, scores, NEGATIVE)
            top = jnp.max(scores, axis=0, keepdims=True)
            raised = jnp.exp(scores - top)
            prob = raised / jnp.sum(raised, axis=0, keepdims=True)
            prob_ref[0, h] = prob
            part = contract(prob.astype(BF16), values[half], (0, 0))
            mixed[b] = part if mixed[b] is None else mixed[b] + part
    for b in range(8):
        stop = min(b * LANES + LANES, D)
        mixed_ref[:, b * LANES : stop] = mixed[b].astype(BF16)[:, : stop - b * LANES]


def attend_back_kernel(heads_ref, prob_ref, dmixed_ref, cos_ref, sin_ref, out_ref):
    lanes = lane_ids(ROWS)
    left = lanes < HEAD
    low_half = (lanes % HEAD) < 32
    cos = cos_ref[...]
    sin = sin_ref[...]
    blocks = [block_of(heads_ref, b, QKV) for b in range(BLOCKS)]
    dmixed = [block_of(dmixed_ref, b, D) for b in range(8)]
    outs = [None] * BLOCKS

    def add(index, term):
        outs[index] = term if outs[index] is None else outs[index] + term

    for kk in range(KV_HEADS):
        kslot, vslot = HEADS + kk, HEADS + KV_HEADS + kk
        keys = both_halves(blocks[kslot // 2].astype(F32), kslot % 2, left)
        values = both_halves(blocks[vslot // 2].astype(F32), vslot % 2, left)
        dkeys = [None, None]
        dvalues = [None, None]
        for h in range(kk * GROUP, kk * GROUP + GROUP):
            half, b = h % 2, h // 2
            prob = prob_ref[0, h]
            dprob = contract(values[half], dmixed[b], (1, 1))
            inner = jnp.sum(dprob * prob, axis=0, keepdims=True)
            dscore = (prob * (dprob - inner)).astype(BF16)
            add(b, contract(dscore, keys[half], (0, 0)))
            dk = contract(dscore, blocks[b], (1, 0))
            dv = contract(prob.astype(BF16), dmixed[b], (1, 0))
            dkeys[half] = dk if dkeys[half] is None else dkeys[half] + dk
            dvalues[half] = dv if dvalues[half] is None else dvalues[half] + dv
        for slot, (low, high) in ((kslot, dkeys), (vslot, dvalues)):
            low = jnp.where(left, low, 0.0)
            high = jnp.where(left, 0.0, high)
            if slot % 2 == 0:
                term = low + pltpu.roll(high, HEAD, 1)
            else:
                term = pltpu.roll(low, HEAD, 1) + high
            add(slot // 2, term)
    for b in range(BLOCKS):
        x = outs[b]
        if b < 10:
            x = x * HEAD_SCALE
            x = x * cos - swapped_halves(x, low_half) * sin
        stop = min(b * LANES + LANES, QKV)
        out_ref[:, b * LANES : stop] = x.astype(BF16)[:, : stop - b * LANES]


def row_spec(width):
    return pl.BlockSpec((ROWS, width), lambda i: (i, 0))


def attend(projected, mask, cos, sin):
    count = mask.shape[0]
    rows = count * ROWS
    return pl.pallas_call(
        attend_kernel,
        grid=(count,),
        in_specs=[
            row_spec(QKV),
            pl.BlockSpec((1, ROWS, ROWS), lambda i: (i, 0, 0)),
            row_spec(LANES),
            row_spec(LANES),
        ],
        out_specs=[
            row_spec(QKV),
            pl.BlockSpec((1, HEADS, ROWS, ROWS), lambda i: (i, 0, 0, 0)),
            row_spec(D),
        ],
        out_shape=[
            jax.ShapeDtypeStruct((rows, QKV), BF16),
            jax.ShapeDtypeStruct((count, HEADS, ROWS, ROWS), F32),
            jax.ShapeDtypeStruct((rows, D), BF16),
        ],
        compiler_params=pltpu.CompilerParams(vmem_limit_bytes=VMEM_LIMIT),
        name="attend",
    )(projected, mask, cos, sin)


def attend_back(heads, prob, dmixed, cos, sin):
    count = prob.shape[0]
    rows = count * ROWS
    return pl.pallas_call(
        attend_back_kernel,
        grid=(count,),
        in_specs=[
            row_spec(QKV),
            pl.BlockSpec((1, HEADS, ROWS, ROWS), lambda i: (i, 0, 0, 0)),
            row_spec(D),
            row_spec(LANES),
            row_spec(LANES),
        ],
        out_specs=row_spec(QKV),
        out_shape=jax.ShapeDtypeStruct((rows, QKV), BF16),
        compiler_params=pltpu.CompilerParams(vmem_limit_bytes=VMEM_LIMIT),
        name="attend_back",
    )(heads, prob, dmixed, cos, sin)


def tables(segments):
    count, rows = segments.shape
    earlier = jnp.sum((segments[:, None, :] < segments[:, :, None]).astype(jnp.int32), axis=2)
    position = (jnp.arange(rows, dtype=jnp.int32)[None, :] - earlier).astype(F32).reshape(count * rows, 1)
    frequency = ROPE_BASE ** (-jnp.arange(HEAD // 2, dtype=F32) * 2.0 / HEAD)
    angles = position * frequency[None, :]
    cos, sin = jnp.cos(angles), jnp.sin(angles)
    order = jnp.arange(rows, dtype=jnp.int32)
    mask = (segments[:, :, None] == segments[:, None, :]) & (order[:, None] <= order[None, :])[None]
    return (
        jnp.concatenate([cos] * 4, axis=1),
        jnp.concatenate([-sin, sin, -sin, sin], axis=1),
        mask.astype(F32),
    )


def mm(a, b):
    return jnp.dot(a, b, preferred_element_type=F32)


def mmt(a, b):
    return lax.dot_general(a, b, (((1,), (1,)), ((), ())), preferred_element_type=F32)


def layer_forward(stream, gains, weights, table, mm_out=mm, mm_gateup=mm, then=lambda mixed: mixed):
    cos, sin, mask = table
    first_scale = lax.rsqrt(jnp.mean(stream * stream, axis=-1, keepdims=True) + EPSILON)
    attn_norm = (stream * first_scale * gains[0]).astype(BF16)
    projected = mm(attn_norm, weights[0])
    heads, prob, mixed = attend(projected, mask, cos, sin)
    mixed = then(mixed)
    middle = stream + mm_out(mixed, weights[1])
    second_scale = lax.rsqrt(jnp.mean(middle * middle, axis=-1, keepdims=True) + EPSILON)
    ffn_norm = (middle * second_scale * gains[1]).astype(BF16)
    gateup = mm_gateup(ffn_norm, weights[2])
    gate, up = gateup[:, :FF], gateup[:, FF:]
    hidden = (gate * jax.nn.sigmoid(gate) * up).astype(BF16)
    output = middle + mmt(hidden, weights[3])
    return output, (stream, first_scale, attn_norm, heads, prob, mixed, middle, second_scale, ffn_norm, gate, up, hidden)


def norm_back(incoming, gain, scale, normed):
    scaled = incoming * gain
    return scale * (scaled - normed * jnp.mean(scaled * normed, axis=-1, keepdims=True))


def layer_backward(dy, kept, gains, weights, table, grads):
    qkv_w, out_w, gateup_w, down_w = weights
    cos, sin, _ = table
    stream, first_scale, attn_norm, heads, prob, mixed, middle, second_scale, ffn_norm, gate, up, hidden = kept
    dz = dy.astype(BF16)
    dhidden = mm(dz, down_w)
    s = jax.nn.sigmoid(gate)
    dgateup = jnp.concatenate(
        [dhidden * up * s * (1.0 + gate * (1.0 - s)), dhidden * gate * s], axis=1
    ).astype(BF16)
    if grads is not None:
        grads.down(dz)
        made = grads.gateup(dgateup)
    dffn = mmt(dgateup, gateup_w)
    second_normed = middle * second_scale
    dmiddle = dy + norm_back(dffn, gains[1], second_scale, second_normed)
    dbranch = dmiddle.astype(BF16)
    if grads is not None:
        grads.branch(dbranch)
        dbranch, _ = lax.optimization_barrier((dbranch, made))
    dmixed = mmt(dbranch, out_w).astype(BF16)
    dprojected = attend_back(heads, prob, dmixed, cos, sin)
    if grads is not None:
        dprojected = grads.heads(dprojected)
    dattn = mmt(dprojected, qkv_w)
    first_normed = stream * first_scale
    if grads is not None:
        gain_grads = jnp.stack([jnp.sum(dattn * first_normed, axis=0), jnp.sum(dffn * second_normed, axis=0)])
        grads.attention(gain_grads)
    return dmiddle + norm_back(dattn, gains[0], first_scale, first_normed)


def place_kernel(counts, at_ref, *refs):
    out_ref = refs[-1]
    step = pl.program_id(0)
    first = 0
    for ref, count in zip(refs, counts):

        @pl.when((step >= first) & (step < first + count))
        def _(ref=ref):
            out_ref[...] = ref[...]

        first += count


def placed(pieces, counts, at, block, shape, base=None):
    firsts = np.cumsum([0] + list(counts))
    bases = () if base is None else (base,)

    def piece_spec(p):
        start, count = int(firsts[p]), counts[p]
        return pl.BlockSpec(block, lambda i, at_ref: (jnp.clip(i - start, 0, count - 1), 0))

    return pl.pallas_call(
        functools.partial(place_kernel, counts),
        grid_spec=pltpu.PrefetchScalarGridSpec(
            num_scalar_prefetch=1,
            grid=(int(firsts[-1]),),
            in_specs=[piece_spec(p) for p in range(len(pieces))] + [pl.BlockSpec(memory_space=pl.ANY)] * len(bases),
            out_specs=pl.BlockSpec(block, lambda i, at_ref: (at_ref[0, i], at_ref[1, i])),
        ),
        out_shape=jax.ShapeDtypeStruct(shape, BF16),
        compiler_params=pltpu.CompilerParams(vmem_limit_bytes=VMEM_LIMIT),
        input_output_aliases={1 + len(pieces): 0} if bases else {},
        name="placed",
    )(jnp.stack(at).astype(jnp.int32), *pieces, *bases)


def hidden_outer_kernel(l0_ref, r0_ref, l1_ref, r1_ref, out_ref, total):
    step = pl.program_id(0)

    @pl.when(step == 0)
    def _():
        for s in range(2):
            part = slice(s * (FF // 2), (s + 1) * (FF // 2))
            value = contract(l0_ref[:, part], r0_ref[...], (0, 0)) + contract(l1_ref[:, part], r1_ref[...], (0, 0))
            total[part] = jnp.concatenate([value, jnp.zeros((FF // 2, 32), F32)], axis=1)

    def rows(s, chunk, start, stop):
        at = s * (FF // 2) + chunk * 80
        return total[at + start : at + stop]

    for j in range(3):

        @pl.when(step == j)
        def _(j=j):
            for chunk in range(16):
                if j == 0:
                    group = rows(0, chunk, 0, 64)
                elif j == 1:
                    group = jnp.concatenate([rows(0, chunk, 64, 80), rows(1, chunk, 0, 48)], axis=0)
                else:
                    group = jnp.concatenate([rows(1, chunk, 48, 80), jnp.zeros((32, 512), F32)], axis=0)
                out_ref[chunk * 64 : chunk * 64 + 64] = group.astype(BF16)


def hidden_outer(left, right):
    operands = (left[0], right[0], left[1], right[1])
    return pl.pallas_call(
        hidden_outer_kernel,
        grid=(3,),
        in_specs=[pl.BlockSpec(a.shape, lambda i: (0, 0)) for a in operands],
        out_specs=pl.BlockSpec((1024, 512), lambda i: (0, 5 + i)),
        out_shape=jax.ShapeDtypeStruct((1024, FF + 1536), BF16),
        scratch_shapes=[pltpu.VMEM((FF, 512), F32)],
        compiler_params=pltpu.CompilerParams(vmem_limit_bytes=OUTER_LIMIT),
        name="hidden_outer",
    )(*operands)


def gateup_outer_kernel(l0_ref, r0_ref, l1_ref, r1_ref, base_ref, out_ref):
    total = contract(l0_ref[...], r0_ref[...], (0, 0)) + contract(l1_ref[...], r1_ref[...], (0, 0))
    out_ref[...] = total.astype(BF16)


def gateup_outer(left, right, base):
    rows, tile = left[0].shape[0], 256
    left_spec = pl.BlockSpec((rows, tile), lambda i: (0, i))
    right_spec = pl.BlockSpec((rows, FF), lambda i: (0, 0))
    return pl.pallas_call(
        gateup_outer_kernel,
        grid=(1024 // tile,),
        in_specs=[left_spec, right_spec, left_spec, right_spec, pl.BlockSpec(memory_space=pl.ANY)],
        out_specs=pl.BlockSpec((tile, FF), lambda i: (i, 0)),
        out_shape=jax.ShapeDtypeStruct(base.shape, BF16),
        input_output_aliases={4: 0},
        compiler_params=pltpu.CompilerParams(vmem_limit_bytes=OUTER_LIMIT),
        name="gateup_outer",
    )(left[0], right[0], left[1], right[1], base)


def attention_outer_kernel(m0, b0, m1, b1, a0, p0, a1, p1, pick_ref, gain_ref, out_ref):
    first = contract(m0[...], b0[...], (0, 0)) + contract(m1[...], b1[...], (0, 0))
    second = contract(a0[...], p0[...], (0, 0)) + contract(a1[...], p1[...], (0, 0))
    out_ref[:, :1280] = jnp.concatenate([first, second], axis=1).astype(BF16)
    out_ref[:, 1280:] = contract(pick_ref[...], gain_ref[...], (0, 1)).astype(BF16)


def attention_outer(mixed, dbranch, attn, dprojected, pick, gain_grads):
    rows, depth = mixed[0].shape
    tile = 256

    def left(height):
        return pl.BlockSpec((height, tile), lambda i: (0, i))

    def right(height, width):
        return pl.BlockSpec((height, width), lambda i: (0, 0))

    return pl.pallas_call(
        attention_outer_kernel,
        grid=(depth // tile,),
        in_specs=[left(rows), right(rows, 480)] * 2 + [left(rows), right(rows, 800)] * 2
        + [left(D), right(LANES, D)],
        out_specs=pl.BlockSpec((tile, 1280 + LANES), lambda i: (i, 0)),
        out_shape=jax.ShapeDtypeStruct((depth, 1280 + LANES), BF16),
        compiler_params=pltpu.CompilerParams(vmem_limit_bytes=OUTER_LIMIT),
        name="attention_outer",
    )(mixed[0], dbranch[0], mixed[1], dbranch[1], attn[0], dprojected[0], attn[1], dprojected[1], pick, gain_grads)


class Ring:
    def __init__(self, v, axis, dim):
        self.v, self.axis, self.dim = v, axis, dim
        self.me = lax.axis_index(axis)
        far, after, ahead = self.part(2), self.part(1), self.part(3)
        cut = self.cut = far.shape[0] // 2
        self.low = self.up(jnp.concatenate([far[:cut], after[cut:]], axis=0))
        self.high = self.back(jnp.concatenate([far[cut:], ahead[:cut]], axis=0))

    def up(self, x):
        return lax.ppermute(x, self.axis, [(i, (i + 1) % 4) for i in range(4)])

    def back(self, x):
        return lax.ppermute(x, self.axis, [(i, (i + 3) % 4) for i in range(4)])

    def part(self, step):
        return lax.dynamic_index_in_dim(self.v, (self.me + step) % 4, self.dim, keepdims=False)

    def end(self, dep):
        self.low_end, self.high_end, dep = lax.optimization_barrier((self.low_end, self.high_end, dep))
        return dep

    def passed(self):
        cut = self.cut
        return self.part(1)[:cut] + self.low[:cut], self.part(3)[cut:] + self.high[:cut]

    def second(self, passed):
        self.low_end, self.high_end = self.up(passed[0]), self.back(passed[1])

    def last(self):
        cut, own = self.cut, self.part(0).astype(F32)
        low = own[:cut] + self.low_end.astype(F32) + self.high[cut:].astype(F32)
        high = own[cut:] + self.high_end.astype(F32) + self.low[cut:].astype(F32)
        return jnp.concatenate([low, high], axis=0).astype(BF16)


def row_order():
    pick = np.zeros((D, 1024), np.float32)
    for row in range(D):
        s, rest = divmod(row, 480)
        chunk, i = divmod(rest, 30)
        pick[row, chunk * 64 + s * 32 + i] = 1.0
    return pick


def with_other(x):
    return x, lax.ppermute(x, "core", SWAP)


def owned_kernel(core_ref, own_ref, across_ref, beside_ref, corner_ref, gateup_ref, output_ref, qkv_ref, down_ref, gains_ref):
    here = own_ref[...].astype(F32) + across_ref[...].astype(F32)
    there = beside_ref[...].astype(F32) + corner_ref[...].astype(F32)
    first = core_ref[0] == 0
    low = jnp.where(first, here, there)
    high = jnp.where(first, there, here)

    def columns(start, width, rows):
        return jnp.concatenate([low[:rows, start : start + width], high[:rows, start : start + width]], axis=1)

    gateup_ref[:, 0, :] = columns(0, FF, 15)
    output_ref[:, 0, :] = columns(FF, 480, 15)
    qkv_ref[:, 0, :] = columns(FF + 480, 800, 15)
    at = FF + 1280
    gains_ref[...] = low[:, at : at + LANES] + high[:, at : at + LANES]
    at += LANES
    for j, rows in enumerate((16, 16, 8)):
        down_ref[16 * j : 16 * j + rows] = columns(at + 512 * j, 480, rows)


def owned(core, *parts):
    vmem = pl.BlockSpec(memory_space=pltpu.VMEM)
    shapes = [(15, 1, 2 * FF), (15, 1, D), (15, 1, QKV), (40, D), (16, LANES)]
    return pl.pallas_call(
        owned_kernel,
        in_specs=[pl.BlockSpec(memory_space=pltpu.SMEM)] + [vmem] * 4,
        out_specs=[vmem] * 5,
        out_shape=[jax.ShapeDtypeStruct(shape, F32) for shape in shapes],
        compiler_params=pltpu.CompilerParams(vmem_limit_bytes=VMEM_LIMIT),
        name="owned",
    )(core.reshape(1).astype(jnp.int32), *parts)


class Gradients:
    def __init__(self, kept):
        self.core = lax.axis_index("core") == 0
        self.shard = lax.axis_index("shard") == 0
        self.pick = jnp.asarray(row_order(), BF16)
        attn_norm, mixed, ffn_norm, hidden = kept[2], kept[5], kept[8], kept[11]
        self.hidden = with_other(hidden)
        self.ffn = with_other(mm(ffn_norm, self.pick).astype(BF16))
        self.attn = with_other(mm(attn_norm, self.pick).astype(BF16))
        self.mixed = with_other(mm(mixed, self.pick).astype(BF16))

    def ready(self, dep):
        ffn, attn, mixed = self.ffn[0], self.attn[0], self.mixed[0]
        ffn, attn, mixed, dep = lax.optimization_barrier((ffn, attn, mixed, dep))
        self.ffn, self.attn, self.mixed = (ffn, self.ffn[1]), (attn, self.attn[1]), (mixed, self.mixed[1])
        return dep

    def shared(self, right):
        cut = right.shape[1] // 2
        keep = jnp.where(self.core, right[:, :cut], right[:, cut:])
        give = jnp.where(self.core, right[:, cut:], right[:, :cut])
        return keep, lax.ppermute(give, "core", SWAP)

    def joined(self, parts):
        shard, core = lax.axis_index("shard"), lax.axis_index("core")
        axes = ("shard", "core")

        def part(s, c):
            return lax.dynamic_index_in_dim(parts, 2 * s + c, 0, keepdims=False)

        across = lax.ppermute(part(1 - shard, core), axes, [(0, 2), (2, 0), (1, 3), (3, 1)])
        beside = lax.ppermute(part(shard, 1 - core), axes, [(0, 1), (1, 0), (2, 3), (3, 2)])
        corner = lax.ppermute(part(1 - shard, 1 - core), axes, [(0, 3), (3, 0), (1, 2), (2, 1)])
        return owned(core, part(shard, core), across, beside, corner)

    def down(self, dz):
        self.base = hidden_outer(self.hidden, self.shared(dz))

    def gateup(self, dgateup):
        made = gateup_outer(self.ffn, self.shared(dgateup), self.base)
        self.ffn_piece = lax.psum_scatter(made, ("z", "x"), scatter_dimension=0, tiled=True)
        return made

    def branch(self, dbranch):
        self.dbranch = self.shared(dbranch)

    def heads(self, dprojected):
        self.dprojected = self.shared(dprojected)
        return dprojected

    def attention(self, gain_grads):
        gain_grads = jnp.pad(gain_grads.astype(BF16), ((0, LANES - 2), (0, 0)))
        made = attention_outer(self.mixed, self.dbranch, self.attn, self.dprojected, self.pick, gain_grads)
        width = made.shape[1]
        attention = Ring(made.reshape(4, 4, 64, width), "z", 0)
        attention.second(attention.passed())
        attention = Ring(attention.last(), "x", 0)
        attention.second(attention.passed())
        self.ffn_piece = attention.end(self.ffn_piece)
        self.attention_piece = attention.last()

    def finish(self):
        def by_owner(piece):
            piece = piece.reshape(2, 32, piece.shape[1])
            both = jnp.stack([piece[:, :16], piece[:, 15:31]], axis=1)
            return both.reshape(4, 16, piece.shape[2])

        groups = [self.ffn_piece[:, FF + 512 * j : FF + 512 * j + 512] for j in range(3)]
        tail = jnp.concatenate(groups, axis=0)[:160].reshape(4, 40, 512)
        tail = jnp.pad(tail, ((0, 0), (0, 8), (0, 0)))
        parts = jnp.concatenate(
            [by_owner(self.ffn_piece[:, :FF]), by_owner(self.attention_piece)]
            + [tail[:, 16 * i : 16 * i + 16] for i in range(3)],
            axis=2,
        )
        gateup, output, qkv, down, gains = self.joined(parts)
        flat = lambda a: a.reshape(1, 15, a.shape[2])
        return flat(qkv), flat(output), flat(gateup), down[None], gains[:15, :2].T[None]


def shards(tokens, segments, cotangent, qkv_weight, output_weight, gateup_weight, down_weight, norm_gains):
    leading = lax.axis_index("section") == 0
    first = lax.axis_index("shard") == 0
    rep = lax.axis_index(REP)

    core = lax.axis_index("core")
    shard = lax.axis_index("shard")
    own_out, own_gateup = output_weight[0], gateup_weight[0]
    rows = jnp.concatenate(
        [lax.dynamic_slice_in_dim(w, jnp.minimum(rep * 16, 464), 16, 0) for w in (own_gateup, own_out)], axis=1
    )
    others = lax.all_gather(lax.ppermute(rows, "shard", SWAP), REP, axis=0, tiled=True)
    own_gains = norm_gains[0]
    other_gains = lax.ppermute(own_gains, "shard", SWAP)
    gains = jnp.concatenate(
        [jnp.where(first, own_gains, other_gains), jnp.where(first, other_gains, own_gains)], axis=1
    ).astype(F32)

    def sent(own):
        half = own.shape[0] // 2
        return lax.ppermute(lax.dynamic_slice_in_dim(own, core * half, half, 0), "shard", SWAP)

    def whole(own, got):
        half, width = got.shape
        beside = lax.ppermute(got, "core", SWAP)
        place = 2 * (1 - shard)
        at = jnp.stack([2 * shard, 2 * shard + 1, place + core, place + 1 - core])
        return placed((own, got, beside), (2, 1, 1), (at, at * 0), (half, width), (4 * half, width))

    def own_turned(own):
        depth, width = own.shape
        rows = jnp.arange(4)
        return placed((own,), (4,), (rows, rows * 0 + shard), (depth // 4, width), (depth, 2 * width))

    def whole_turned(base, got):
        half, width = got.shape
        beside = lax.ppermute(got, "core", SWAP)
        rows = jnp.stack([2 * core, 2 * core + 1, 2 - 2 * core, 3 - 2 * core])
        return placed((got, beside), (2, 2), (rows, rows * 0 + 1 - shard), (half // 2, width), base.shape, base)

    def own_first(own, rows):
        at = shard * (480 // rows) + jnp.arange(480 // rows)
        return placed((own,), (480 // rows,), (at, at * 0), (rows, own.shape[1]), (D, own.shape[1]))

    def beside_own(base, other, rows):
        at = (1 - shard) * (480 // rows) + jnp.arange(480 // rows)
        return placed((other,), (480 // rows,), (at, at * 0), (rows, base.shape[1]), base.shape, base)

    def halved(x, pieces):
        cut = D // 2
        own = jnp.where(first, x[:, :cut], x[:, cut:])
        other = jnp.pad(jnp.where(first, x[:, cut:], x[:, :cut]), ((0, 0), (0, 32)))
        return mm(own, pieces[0]) + mm(other, pieces[1])

    turned = down_weight[0].T
    coming = [sent(qkv_weight[0]), sent(turned)]
    qkv_w = whole(qkv_weight[0], coming[0])

    table = tables(segments)
    inputs = tokens.astype(F32)
    down_base, out_base, gateup_base = own_turned(turned), own_first(own_out, 240), own_first(own_gateup, 80)
    parts = [qkv_w, (own_out, others[:, 2 * FF :]), (own_gateup, others[:, : 2 * FF]), None]

    def fetch_down(mixed):
        mixed, got = lax.optimization_barrier((mixed, coming[1]))
        parts[3] = whole_turned(down_base, got)
        return mixed

    early, _ = layer_forward(inputs, gains, parts, table, halved, halved, fetch_down)
    early = early.astype(BF16)
    arrived = lax.ppermute(early, "section", [(0, 1)])
    _, others = lax.optimization_barrier((early, others))
    weights = (qkv_w, beside_own(out_base, others[:, 2 * FF :], 240), beside_own(gateup_base, others, 80), parts[3])
    arrived, weights = lax.optimization_barrier((arrived, weights))
    arrived = arrived.astype(F32)
    stream = jnp.where(leading, inputs, arrived)
    output, kept = layer_forward(stream, gains, weights, table)

    early = layer_backward(cotangent, kept, gains, weights, table, None).astype(BF16)
    arrived = lax.ppermute(early, "section", [(1, 0)])
    _, kept = lax.optimization_barrier((early, kept))
    grads = Gradients(kept)
    arrived = grads.ready(arrived).astype(F32)
    dy = lax.optimization_barrier(jnp.where(leading, arrived, cotangent))
    down = layer_backward(dy, kept, gains, weights, table, grads)
    return (output[None], down[None], *grads.finish())


def solution(mesh):
    sizes = mesh.shape
    fine = Mesh(
        mesh.devices.reshape(sizes["section"], sizes["shard"], 4, 4, 2),
        ("section", "shard", "z", "x", "core"),
    )
    tokens = ("shard",) + REP
    in_specs = (
        P(tokens, None),
        P(tokens, None),
        P(tokens, None),
        P("section", "shard", None),
        P("section", "shard", None),
        P("section", "shard", None),
        P("section", "shard", None),
        P("section", None, "shard"),
    )
    out_specs = (
        P("section", tokens, None),
        P("section", tokens, None),
        P("section", tokens, None),
        P("section", tokens, None),
        P("section", tokens, None),
        P("section", tokens, None),
        P("section", None, tokens),
    )
    return jax.shard_map(shards, mesh=fine, in_specs=in_specs, out_specs=out_specs, check_vma=False)
```

```python
import functools

import jax
import jax.numpy as jnp
import numpy as np
from jax import lax
from jax.experimental import pallas as pl
from jax.experimental.pallas import tpu as pltpu
from jax.sharding import Mesh
from jax.sharding import PartitionSpec as P

D = 960
HEADS = 15
KV_HEADS = 5
GROUP = HEADS // KV_HEADS
HEAD = 64
FF = 2560
QKV = 1600
ROWS = 112
LANES = 128
BLOCKS = 13
EPSILON = 1e-05
ROPE_BASE = 100000.0
NEGATIVE = -1e30
HEAD_SCALE = HEAD ** (-0.5)
BF16 = jnp.bfloat16
F32 = jnp.float32
REP = ("z", "x", "core")
SWAP = [(0, 1), (1, 0)]
VMEM_LIMIT = 12 * 1024 * 1024
OUTER_LIMIT = 20 * 1024 * 1024


def lane_ids(rows):
    return lax.broadcasted_iota(jnp.int32, (rows, LANES), 1)


def swapped_halves(x, low_half):
    return jnp.where(low_half, pltpu.roll(x, LANES - 32, 1), pltpu.roll(x, 32, 1))


def block_of(ref, index, width):
    start = index * LANES
    stop = min(start + LANES, width)
    part = ref[:, start:stop]
    if stop - start < LANES:
        part = jnp.concatenate([part, jnp.zeros((part.shape[0], LANES - (stop - start)), part.dtype)], axis=1)
    return part


def both_halves(block, slot, left):
    if slot == 0:
        low = jnp.where(left, block, 0.0)
        high = pltpu.roll(low, HEAD, 1)
    else:
        high = jnp.where(left, 0.0, block)
        low = pltpu.roll(high, HEAD, 1)
    return low.astype(BF16), high.astype(BF16)


def contract(a, b, dims):
    return lax.dot_general(a, b, ((dims[0:1], dims[1:2]), ((), ())), preferred_element_type=F32)


def attend_kernel(proj_ref, mask_ref, cos_ref, sin_ref, heads_ref, prob_ref, mixed_ref):
    lanes = lane_ids(ROWS)
    left = lanes < HEAD
    low_half = (lanes % HEAD) < 32
    cos = cos_ref[...]
    sin = sin_ref[...]
    mask = mask_ref[0] > 0.0
    blocks = []
    for b in range(BLOCKS):
        x = block_of(proj_ref, b, QKV)
        if b < 10:
            x = x * cos + swapped_halves(x, low_half) * sin
        low = x.astype(BF16)
        blocks.append(low)
        stop = min(b * LANES + LANES, QKV)
        heads_ref[:, b * LANES : stop] = low[:, : stop - b * LANES]
    mixed = [None] * 8
    for kk in range(KV_HEADS):
        kslot, vslot = HEADS + kk, HEADS + KV_HEADS + kk
        keys = both_halves(blocks[kslot // 2].astype(F32), kslot % 2, left)
        values = both_halves(blocks[vslot // 2].astype(F32), vslot % 2, left)
        for h in range(kk * GROUP, kk * GROUP + GROUP):
            half, b = h % 2, h // 2
            scores = contract(keys[half], blocks[b], (1, 1)) * HEAD_SCALE
            scores = jnp.where(mask, scores, NEGATIVE)
            top = jnp.max(scores, axis=0, keepdims=True)
            raised = jnp.exp(scores - top)
            prob = raised / jnp.sum(raised, axis=0, keepdims=True)
            prob_ref[0, h] = prob
            part = contract(prob.astype(BF16), values[half], (0, 0))
            mixed[b] = part if mixed[b] is None else mixed[b] + part
    for b in range(8):
        stop = min(b * LANES + LANES, D)
        mixed_ref[:, b * LANES : stop] = mixed[b].astype(BF16)[:, : stop - b * LANES]


def attend_back_kernel(heads_ref, prob_ref, dmixed_ref, cos_ref, sin_ref, out_ref):
    lanes = lane_ids(ROWS)
    left = lanes < HEAD
    low_half = (lanes % HEAD) < 32
    cos = cos_ref[...]
    sin = sin_ref[...]
    blocks = [block_of(heads_ref, b, QKV) for b in range(BLOCKS)]
    dmixed = [block_of(dmixed_ref, b, D) for b in range(8)]
    outs = [None] * BLOCKS

    def add(index, term):
        outs[index] = term if outs[index] is None else outs[index] + term

    for kk in range(KV_HEADS):
        kslot, vslot = HEADS + kk, HEADS + KV_HEADS + kk
        keys = both_halves(blocks[kslot // 2].astype(F32), kslot % 2, left)
        values = both_halves(blocks[vslot // 2].astype(F32), vslot % 2, left)
        dkeys = [None, None]
        dvalues = [None, None]
        for h in range(kk * GROUP, kk * GROUP + GROUP):
            half, b = h % 2, h // 2
            prob = prob_ref[0, h]
            dprob = contract(values[half], dmixed[b], (1, 1))
            inner = jnp.sum(dprob * prob, axis=0, keepdims=True)
            dscore = (prob * (dprob - inner)).astype(BF16)
            add(b, contract(dscore, keys[half], (0, 0)))
            dk = contract(dscore, blocks[b], (1, 0))
            dv = contract(prob.astype(BF16), dmixed[b], (1, 0))
            dkeys[half] = dk if dkeys[half] is None else dkeys[half] + dk
            dvalues[half] = dv if dvalues[half] is None else dvalues[half] + dv
        for slot, (low, high) in ((kslot, dkeys), (vslot, dvalues)):
            low = jnp.where(left, low, 0.0)
            high = jnp.where(left, 0.0, high)
            if slot % 2 == 0:
                term = low + pltpu.roll(high, HEAD, 1)
            else:
                term = pltpu.roll(low, HEAD, 1) + high
            add(slot // 2, term)
    for b in range(BLOCKS):
        x = outs[b]
        if b < 10:
            x = x * HEAD_SCALE
            x = x * cos - swapped_halves(x, low_half) * sin
        stop = min(b * LANES + LANES, QKV)
        out_ref[:, b * LANES : stop] = x.astype(BF16)[:, : stop - b * LANES]


def row_spec(width):
    return pl.BlockSpec((ROWS, width), lambda i: (i, 0))


def attend(projected, mask, cos, sin):
    count = mask.shape[0]
    rows = count * ROWS
    return pl.pallas_call(
        attend_kernel,
        grid=(count,),
        in_specs=[
            row_spec(QKV),
            pl.BlockSpec((1, ROWS, ROWS), lambda i: (i, 0, 0)),
            row_spec(LANES),
            row_spec(LANES),
        ],
        out_specs=[
            row_spec(QKV),
            pl.BlockSpec((1, HEADS, ROWS, ROWS), lambda i: (i, 0, 0, 0)),
            row_spec(D),
        ],
        out_shape=[
            jax.ShapeDtypeStruct((rows, QKV), BF16),
            jax.ShapeDtypeStruct((count, HEADS, ROWS, ROWS), F32),
            jax.ShapeDtypeStruct((rows, D), BF16),
        ],
        compiler_params=pltpu.CompilerParams(vmem_limit_bytes=VMEM_LIMIT),
        name="attend",
    )(projected, mask, cos, sin)


def attend_back(heads, prob, dmixed, cos, sin):
    count = prob.shape[0]
    rows = count * ROWS
    return pl.pallas_call(
        attend_back_kernel,
        grid=(count,),
        in_specs=[
            row_spec(QKV),
            pl.BlockSpec((1, HEADS, ROWS, ROWS), lambda i: (i, 0, 0, 0)),
            row_spec(D),
            row_spec(LANES),
            row_spec(LANES),
        ],
        out_specs=row_spec(QKV),
        out_shape=jax.ShapeDtypeStruct((rows, QKV), BF16),
        compiler_params=pltpu.CompilerParams(vmem_limit_bytes=VMEM_LIMIT),
        name="attend_back",
    )(heads, prob, dmixed, cos, sin)


def tables(segments):
    count, rows = segments.shape
    earlier = jnp.sum((segments[:, None, :] < segments[:, :, None]).astype(jnp.int32), axis=2)
    position = (jnp.arange(rows, dtype=jnp.int32)[None, :] - earlier).astype(F32).reshape(count * rows, 1)
    frequency = ROPE_BASE ** (-jnp.arange(HEAD // 2, dtype=F32) * 2.0 / HEAD)
    angles = position * frequency[None, :]
    cos, sin = jnp.cos(angles), jnp.sin(angles)
    order = jnp.arange(rows, dtype=jnp.int32)
    mask = (segments[:, :, None] == segments[:, None, :]) & (order[:, None] <= order[None, :])[None]
    return (
        jnp.concatenate([cos] * 4, axis=1),
        jnp.concatenate([-sin, sin, -sin, sin], axis=1),
        mask.astype(F32),
    )


def mm(a, b):
    return jnp.dot(a, b, preferred_element_type=F32)


def mmt(a, b):
    return lax.dot_general(a, b, (((1,), (1,)), ((), ())), preferred_element_type=F32)


def layer_forward(stream, gains, weights, table, mm_out=mm, mm_gateup=mm, then=lambda mixed: mixed):
    cos, sin, mask = table
    first_scale = lax.rsqrt(jnp.mean(stream * stream, axis=-1, keepdims=True) + EPSILON)
    attn_norm = (stream * first_scale * gains[0]).astype(BF16)
    projected = mm(attn_norm, weights[0])
    heads, prob, mixed = attend(projected, mask, cos, sin)
    mixed = then(mixed)
    middle = stream + mm_out(mixed, weights[1])
    second_scale = lax.rsqrt(jnp.mean(middle * middle, axis=-1, keepdims=True) + EPSILON)
    ffn_norm = (middle * second_scale * gains[1]).astype(BF16)
    gateup = mm_gateup(ffn_norm, weights[2])
    gate, up = gateup[:, :FF], gateup[:, FF:]
    hidden = (gate * jax.nn.sigmoid(gate) * up).astype(BF16)
    output = middle + mmt(hidden, weights[3])
    return output, (stream, first_scale, attn_norm, heads, prob, mixed, middle, second_scale, ffn_norm, gate, up, hidden)


def norm_back(incoming, gain, scale, normed):
    scaled = incoming * gain
    return scale * (scaled - normed * jnp.mean(scaled * normed, axis=-1, keepdims=True))


def middle_back_kernel(dgateup_ref, weight_ref, middle_ref, scale_ref, gain_ref, dy_ref, dmiddle_ref, dbranch_ref, sum_ref, total):
    step = pl.program_id(0)
    part = contract(dgateup_ref[...], weight_ref[...], (1, 1))

    @pl.when(step == 0)
    def _():
        total[...] = part

    @pl.when(step > 0)
    def _():
        total[...] += part

    @pl.when(step == pl.num_programs(0) - 1)
    def _():
        incoming, scale = total[...], scale_ref[...]
        normed = middle_ref[...] * scale
        scaled = incoming * gain_ref[...]
        mean = jnp.mean(scaled * normed, axis=-1, keepdims=True)
        dmiddle = dy_ref[...] + scale * (scaled - normed * mean)
        dmiddle_ref[...] = dmiddle
        dbranch_ref[...] = dmiddle.astype(BF16)
        sum_ref[...] = jnp.sum(incoming * normed, axis=0, keepdims=True)


def middle_back(dgateup, weight, middle, scale, gain, dy):
    rows, tile = dgateup.shape[0], 512

    def full(a):
        return pl.BlockSpec(a.shape, lambda k: (0, 0))

    return pl.pallas_call(
        middle_back_kernel,
        grid=(2 * FF // tile,),
        in_specs=[
            pl.BlockSpec((rows, tile), lambda k: (0, k)),
            pl.BlockSpec((D, tile), lambda k: (0, k)),
            full(middle),
            full(scale),
            full(gain),
            full(dy),
        ],
        out_specs=[full(middle), full(middle), full(gain)],
        out_shape=[
            jax.ShapeDtypeStruct(middle.shape, F32),
            jax.ShapeDtypeStruct(middle.shape, BF16),
            jax.ShapeDtypeStruct(gain.shape, F32),
        ],
        scratch_shapes=[pltpu.VMEM(middle.shape, F32)],
        compiler_params=pltpu.CompilerParams(vmem_limit_bytes=VMEM_LIMIT),
        name="middle_back",
    )(dgateup, weight, middle, scale, gain, dy)


def layer_backward(dy, kept, gains, weights, table, grads):
    qkv_w, out_w, gateup_w, down_w = weights
    cos, sin, _ = table
    stream, first_scale, attn_norm, heads, prob, mixed, middle, second_scale, ffn_norm, gate, up, hidden = kept
    dz = dy.astype(BF16)
    dhidden = mm(dz, down_w)
    s = jax.nn.sigmoid(gate)
    dgateup = jnp.concatenate(
        [dhidden * up * s * (1.0 + gate * (1.0 - s)), dhidden * gate * s], axis=1
    ).astype(BF16)
    if grads is not None:
        grads.down(dz)
        made = grads.gateup(dgateup)
    dmiddle, dbranch, second_sum = middle_back(dgateup, gateup_w, middle, second_scale, gains[1:2], dy)
    if grads is not None:
        grads.branch(dbranch)
        dbranch, _ = lax.optimization_barrier((dbranch, made))
    dmixed = mmt(dbranch, out_w).astype(BF16)
    dprojected = attend_back(heads, prob, dmixed, cos, sin)
    if grads is not None:
        dprojected = grads.heads(dprojected)
    dattn = mmt(dprojected, qkv_w)
    first_normed = stream * first_scale
    if grads is not None:
        gain_grads = jnp.stack([jnp.sum(dattn * first_normed, axis=0), second_sum[0]])
        grads.attention(gain_grads)
    return dmiddle + norm_back(dattn, gains[0], first_scale, first_normed)


def place_kernel(counts, at_ref, *refs):
    out_ref = refs[-1]
    step = pl.program_id(0)
    first = 0
    for ref, count in zip(refs, counts):

        @pl.when((step >= first) & (step < first + count))
        def _(ref=ref):
            out_ref[...] = ref[...]

        first += count


def placed(pieces, counts, at, block, shape, base=None):
    firsts = np.cumsum([0] + list(counts))
    bases = () if base is None else (base,)

    def piece_spec(p):
        start, count = int(firsts[p]), counts[p]
        return pl.BlockSpec(block, lambda i, at_ref: (jnp.clip(i - start, 0, count - 1), 0))

    return pl.pallas_call(
        functools.partial(place_kernel, counts),
        grid_spec=pltpu.PrefetchScalarGridSpec(
            num_scalar_prefetch=1,
            grid=(int(firsts[-1]),),
            in_specs=[piece_spec(p) for p in range(len(pieces))] + [pl.BlockSpec(memory_space=pl.ANY)] * len(bases),
            out_specs=pl.BlockSpec(block, lambda i, at_ref: (at_ref[0, i], at_ref[1, i])),
        ),
        out_shape=jax.ShapeDtypeStruct(shape, BF16),
        compiler_params=pltpu.CompilerParams(vmem_limit_bytes=VMEM_LIMIT),
        input_output_aliases={1 + len(pieces): 0} if bases else {},
        name="placed",
    )(jnp.stack(at).astype(jnp.int32), *pieces, *bases)


def hidden_outer_kernel(l0_ref, r0_ref, l1_ref, r1_ref, out_ref, total):
    step = pl.program_id(0)

    @pl.when(step == 0)
    def _():
        for s in range(2):
            part = slice(s * (FF // 2), (s + 1) * (FF // 2))
            value = contract(l0_ref[:, part], r0_ref[...], (0, 0)) + contract(l1_ref[:, part], r1_ref[...], (0, 0))
            total[part] = jnp.concatenate([value, jnp.zeros((FF // 2, 32), F32)], axis=1)

    def rows(s, chunk, start, stop):
        at = s * (FF // 2) + chunk * 80
        return total[at + start : at + stop]

    for j in range(3):

        @pl.when(step == j)
        def _(j=j):
            for chunk in range(16):
                if j == 0:
                    group = rows(0, chunk, 0, 64)
                elif j == 1:
                    group = jnp.concatenate([rows(0, chunk, 64, 80), rows(1, chunk, 0, 48)], axis=0)
                else:
                    group = jnp.concatenate([rows(1, chunk, 48, 80), jnp.zeros((32, 512), F32)], axis=0)
                out_ref[chunk * 64 : chunk * 64 + 64] = group.astype(BF16)


def hidden_outer(left, right):
    operands = (left[0], right[0], left[1], right[1])
    return pl.pallas_call(
        hidden_outer_kernel,
        grid=(3,),
        in_specs=[pl.BlockSpec(a.shape, lambda i: (0, 0)) for a in operands],
        out_specs=pl.BlockSpec((1024, 512), lambda i: (0, 5 + i)),
        out_shape=jax.ShapeDtypeStruct((1024, FF + 1536), BF16),
        scratch_shapes=[pltpu.VMEM((FF, 512), F32)],
        compiler_params=pltpu.CompilerParams(vmem_limit_bytes=OUTER_LIMIT),
        name="hidden_outer",
    )(*operands)


def gateup_outer_kernel(l0_ref, r0_ref, l1_ref, r1_ref, base_ref, out_ref):
    total = contract(l0_ref[...], r0_ref[...], (0, 0)) + contract(l1_ref[...], r1_ref[...], (0, 0))
    out_ref[...] = total.astype(BF16)


def gateup_outer(left, right, base):
    rows, tile = left[0].shape[0], 256
    left_spec = pl.BlockSpec((rows, tile), lambda i: (0, i))
    right_spec = pl.BlockSpec((rows, FF), lambda i: (0, 0))
    return pl.pallas_call(
        gateup_outer_kernel,
        grid=(1024 // tile,),
        in_specs=[left_spec, right_spec, left_spec, right_spec, pl.BlockSpec(memory_space=pl.ANY)],
        out_specs=pl.BlockSpec((tile, FF), lambda i: (i, 0)),
        out_shape=jax.ShapeDtypeStruct(base.shape, BF16),
        input_output_aliases={4: 0},
        compiler_params=pltpu.CompilerParams(vmem_limit_bytes=OUTER_LIMIT),
        name="gateup_outer",
    )(left[0], right[0], left[1], right[1], base)


def attention_outer_kernel(m0, b0, m1, b1, a0, p0, a1, p1, pick_ref, gain_ref, out_ref):
    first = contract(m0[...], b0[...], (0, 0)) + contract(m1[...], b1[...], (0, 0))
    second = contract(a0[...], p0[...], (0, 0)) + contract(a1[...], p1[...], (0, 0))
    out_ref[:, :1280] = jnp.concatenate([first, second], axis=1).astype(BF16)
    out_ref[:, 1280:] = contract(pick_ref[...], gain_ref[...], (0, 1)).astype(BF16)


def attention_outer(mixed, dbranch, attn, dprojected, pick, gain_grads):
    rows, depth = mixed[0].shape
    tile = 256

    def left(height):
        return pl.BlockSpec((height, tile), lambda i: (0, i))

    def right(height, width):
        return pl.BlockSpec((height, width), lambda i: (0, 0))

    return pl.pallas_call(
        attention_outer_kernel,
        grid=(depth // tile,),
        in_specs=[left(rows), right(rows, 480)] * 2 + [left(rows), right(rows, 800)] * 2
        + [left(D), right(LANES, D)],
        out_specs=pl.BlockSpec((tile, 1280 + LANES), lambda i: (i, 0)),
        out_shape=jax.ShapeDtypeStruct((depth, 1280 + LANES), BF16),
        compiler_params=pltpu.CompilerParams(vmem_limit_bytes=OUTER_LIMIT),
        name="attention_outer",
    )(mixed[0], dbranch[0], mixed[1], dbranch[1], attn[0], dprojected[0], attn[1], dprojected[1], pick, gain_grads)


class Ring:
    def __init__(self, v, axis, dim):
        self.v, self.axis, self.dim = v, axis, dim
        self.me = lax.axis_index(axis)
        far, after, ahead = self.part(2), self.part(1), self.part(3)
        cut = self.cut = far.shape[0] // 2
        self.low = self.up(jnp.concatenate([far[:cut], after[cut:]], axis=0))
        self.high = self.back(jnp.concatenate([far[cut:], ahead[:cut]], axis=0))

    def up(self, x):
        return lax.ppermute(x, self.axis, [(i, (i + 1) % 4) for i in range(4)])

    def back(self, x):
        return lax.ppermute(x, self.axis, [(i, (i + 3) % 4) for i in range(4)])

    def part(self, step):
        return lax.dynamic_index_in_dim(self.v, (self.me + step) % 4, self.dim, keepdims=False)

    def end(self, dep):
        self.low_end, self.high_end, dep = lax.optimization_barrier((self.low_end, self.high_end, dep))
        return dep

    def passed(self):
        cut = self.cut
        return self.part(1)[:cut] + self.low[:cut], self.part(3)[cut:] + self.high[:cut]

    def second(self, passed):
        self.low_end, self.high_end = self.up(passed[0]), self.back(passed[1])

    def last(self):
        cut, own = self.cut, self.part(0).astype(F32)
        low = own[:cut] + self.low_end.astype(F32) + self.high[cut:].astype(F32)
        high = own[cut:] + self.high_end.astype(F32) + self.low[cut:].astype(F32)
        return jnp.concatenate([low, high], axis=0).astype(BF16)


def row_order():
    pick = np.zeros((D, 1024), np.float32)
    for row in range(D):
        s, rest = divmod(row, 480)
        chunk, i = divmod(rest, 30)
        pick[row, chunk * 64 + s * 32 + i] = 1.0
    return pick


def with_other(x):
    return x, lax.ppermute(x, "core", SWAP)


def owned_kernel(core_ref, own_ref, across_ref, beside_ref, corner_ref, gateup_ref, output_ref, qkv_ref, down_ref, gains_ref):
    here = own_ref[...].astype(F32) + across_ref[...].astype(F32)
    there = beside_ref[...].astype(F32) + corner_ref[...].astype(F32)
    first = core_ref[0] == 0
    low = jnp.where(first, here, there)
    high = jnp.where(first, there, here)

    def columns(start, width, rows):
        return jnp.concatenate([low[:rows, start : start + width], high[:rows, start : start + width]], axis=1)

    gateup_ref[:, 0, :] = columns(0, FF, 15)
    output_ref[:, 0, :] = columns(FF, 480, 15)
    qkv_ref[:, 0, :] = columns(FF + 480, 800, 15)
    at = FF + 1280
    gains_ref[...] = low[:, at : at + LANES] + high[:, at : at + LANES]
    at += LANES
    for j, rows in enumerate((16, 16, 8)):
        down_ref[16 * j : 16 * j + rows] = columns(at + 512 * j, 480, rows)


def owned(core, *parts):
    vmem = pl.BlockSpec(memory_space=pltpu.VMEM)
    shapes = [(15, 1, 2 * FF), (15, 1, D), (15, 1, QKV), (40, D), (16, LANES)]
    return pl.pallas_call(
        owned_kernel,
        in_specs=[pl.BlockSpec(memory_space=pltpu.SMEM)] + [vmem] * 4,
        out_specs=[vmem] * 5,
        out_shape=[jax.ShapeDtypeStruct(shape, F32) for shape in shapes],
        compiler_params=pltpu.CompilerParams(vmem_limit_bytes=VMEM_LIMIT),
        name="owned",
    )(core.reshape(1).astype(jnp.int32), *parts)


class Gradients:
    def __init__(self, kept):
        self.core = lax.axis_index("core") == 0
        self.shard = lax.axis_index("shard") == 0
        self.pick = jnp.asarray(row_order(), BF16)
        attn_norm, mixed, ffn_norm, hidden = kept[2], kept[5], kept[8], kept[11]
        self.hidden = with_other(hidden)
        self.ffn = with_other(mm(ffn_norm, self.pick).astype(BF16))
        self.attn = with_other(mm(attn_norm, self.pick).astype(BF16))
        self.mixed = with_other(mm(mixed, self.pick).astype(BF16))

    def ready(self, dep):
        ffn, attn, mixed = self.ffn[0], self.attn[0], self.mixed[0]
        ffn, attn, mixed, dep = lax.optimization_barrier((ffn, attn, mixed, dep))
        self.ffn, self.attn, self.mixed = (ffn, self.ffn[1]), (attn, self.attn[1]), (mixed, self.mixed[1])
        return dep

    def shared(self, right):
        cut = right.shape[1] // 2
        keep = jnp.where(self.core, right[:, :cut], right[:, cut:])
        give = jnp.where(self.core, right[:, cut:], right[:, :cut])
        return keep, lax.ppermute(give, "core", SWAP)

    def joined(self, parts):
        shard, core = lax.axis_index("shard"), lax.axis_index("core")
        axes = ("shard", "core")

        def part(s, c):
            return lax.dynamic_index_in_dim(parts, 2 * s + c, 0, keepdims=False)

        across = lax.ppermute(part(1 - shard, core), axes, [(0, 2), (2, 0), (1, 3), (3, 1)])
        beside = lax.ppermute(part(shard, 1 - core), axes, [(0, 1), (1, 0), (2, 3), (3, 2)])
        corner = lax.ppermute(part(1 - shard, 1 - core), axes, [(0, 3), (3, 0), (1, 2), (2, 1)])
        return owned(core, part(shard, core), across, beside, corner)

    def down(self, dz):
        self.base = hidden_outer(self.hidden, self.shared(dz))

    def gateup(self, dgateup):
        made = gateup_outer(self.ffn, self.shared(dgateup), self.base)
        self.ffn_piece = lax.psum_scatter(made, ("z", "x"), scatter_dimension=0, tiled=True)
        return made

    def branch(self, dbranch):
        self.dbranch = self.shared(dbranch)

    def heads(self, dprojected):
        self.dprojected = self.shared(dprojected)
        return dprojected

    def attention(self, gain_grads):
        gain_grads = jnp.pad(gain_grads.astype(BF16), ((0, LANES - 2), (0, 0)))
        made = attention_outer(self.mixed, self.dbranch, self.attn, self.dprojected, self.pick, gain_grads)
        width = made.shape[1]
        attention = Ring(made.reshape(4, 4, 64, width), "z", 0)
        attention.second(attention.passed())
        attention = Ring(attention.last(), "x", 0)
        attention.second(attention.passed())
        self.ffn_piece = attention.end(self.ffn_piece)
        self.attention_piece = attention.last()

    def finish(self):
        def by_owner(piece):
            piece = piece.reshape(2, 32, piece.shape[1])
            both = jnp.stack([piece[:, :16], piece[:, 15:31]], axis=1)
            return both.reshape(4, 16, piece.shape[2])

        groups = [self.ffn_piece[:, FF + 512 * j : FF + 512 * j + 512] for j in range(3)]
        tail = jnp.concatenate(groups, axis=0)[:160].reshape(4, 40, 512)
        tail = jnp.pad(tail, ((0, 0), (0, 8), (0, 0)))
        parts = jnp.concatenate(
            [by_owner(self.ffn_piece[:, :FF]), by_owner(self.attention_piece)]
            + [tail[:, 16 * i : 16 * i + 16] for i in range(3)],
            axis=2,
        )
        gateup, output, qkv, down, gains = self.joined(parts)
        flat = lambda a: a.reshape(1, 15, a.shape[2])
        return flat(qkv), flat(output), flat(gateup), down[None], gains[:15, :2].T[None]


def shards(tokens, segments, cotangent, qkv_weight, output_weight, gateup_weight, down_weight, norm_gains):
    leading = lax.axis_index("section") == 0
    first = lax.axis_index("shard") == 0
    rep = lax.axis_index(REP)

    core = lax.axis_index("core")
    shard = lax.axis_index("shard")
    own_out, own_gateup = output_weight[0], gateup_weight[0]
    rows = jnp.concatenate(
        [lax.dynamic_slice_in_dim(w, jnp.minimum(rep * 16, 464), 16, 0) for w in (own_gateup, own_out)], axis=1
    )
    others = lax.all_gather(lax.ppermute(rows, "shard", SWAP), REP, axis=0, tiled=True)
    own_gains = norm_gains[0]
    other_gains = lax.ppermute(own_gains, "shard", SWAP)
    gains = jnp.concatenate(
        [jnp.where(first, own_gains, other_gains), jnp.where(first, other_gains, own_gains)], axis=1
    ).astype(F32)

    def sent(own):
        half = own.shape[0] // 2
        return lax.ppermute(lax.dynamic_slice_in_dim(own, core * half, half, 0), "shard", SWAP)

    def whole(own, got):
        half, width = got.shape
        beside = lax.ppermute(got, "core", SWAP)
        place = 2 * (1 - shard)
        at = jnp.stack([2 * shard, 2 * shard + 1, place + core, place + 1 - core])
        return placed((own, got, beside), (2, 1, 1), (at, at * 0), (half, width), (4 * half, width))

    def own_turned(own):
        depth, width = own.shape
        rows = jnp.arange(4)
        return placed((own,), (4,), (rows, rows * 0 + shard), (depth // 4, width), (depth, 2 * width))

    def whole_turned(base, got):
        half, width = got.shape
        beside = lax.ppermute(got, "core", SWAP)
        rows = jnp.stack([2 * core, 2 * core + 1, 2 - 2 * core, 3 - 2 * core])
        return placed((got, beside), (2, 2), (rows, rows * 0 + 1 - shard), (half // 2, width), base.shape, base)

    def own_first(own, rows):
        at = shard * (480 // rows) + jnp.arange(480 // rows)
        return placed((own,), (480 // rows,), (at, at * 0), (rows, own.shape[1]), (D, own.shape[1]))

    def beside_own(base, other, rows):
        at = (1 - shard) * (480 // rows) + jnp.arange(480 // rows)
        return placed((other,), (480 // rows,), (at, at * 0), (rows, base.shape[1]), base.shape, base)

    def halved(x, pieces):
        cut = D // 2
        own = jnp.where(first, x[:, :cut], x[:, cut:])
        other = jnp.pad(jnp.where(first, x[:, cut:], x[:, :cut]), ((0, 0), (0, 32)))
        return mm(own, pieces[0]) + mm(other, pieces[1])

    turned = down_weight[0].T
    coming = [sent(qkv_weight[0]), sent(turned)]
    qkv_w = whole(qkv_weight[0], coming[0])

    table = tables(segments)
    inputs = tokens.astype(F32)
    down_base, out_base, gateup_base = own_turned(turned), own_first(own_out, 240), own_first(own_gateup, 80)
    parts = [qkv_w, (own_out, others[:, 2 * FF :]), (own_gateup, others[:, : 2 * FF]), None]

    def fetch_down(mixed):
        mixed, got = lax.optimization_barrier((mixed, coming[1]))
        parts[3] = whole_turned(down_base, got)
        return mixed

    early, _ = layer_forward(inputs, gains, parts, table, halved, halved, fetch_down)
    early = early.astype(BF16)
    arrived = lax.ppermute(early, "section", [(0, 1)])
    _, others = lax.optimization_barrier((early, others))
    weights = (qkv_w, beside_own(out_base, others[:, 2 * FF :], 240), beside_own(gateup_base, others, 80), parts[3])
    arrived, weights = lax.optimization_barrier((arrived, weights))
    arrived = arrived.astype(F32)
    stream = jnp.where(leading, inputs, arrived)
    output, kept = layer_forward(stream, gains, weights, table)

    early = layer_backward(cotangent, kept, gains, weights, table, None).astype(BF16)
    arrived = lax.ppermute(early, "section", [(1, 0)])
    _, kept = lax.optimization_barrier((early, kept))
    grads = Gradients(kept)
    arrived = grads.ready(arrived).astype(F32)
    dy = lax.optimization_barrier(jnp.where(leading, arrived, cotangent))
    down = layer_backward(dy, kept, gains, weights, table, grads)
    return (output[None], down[None], *grads.finish())


def solution(mesh):
    sizes = mesh.shape
    fine = Mesh(
        mesh.devices.reshape(sizes["section"], sizes["shard"], 4, 4, 2),
        ("section", "shard", "z", "x", "core"),
    )
    tokens = ("shard",) + REP
    in_specs = (
        P(tokens, None),
        P(tokens, None),
        P(tokens, None),
        P("section", "shard", None),
        P("section", "shard", None),
        P("section", "shard", None),
        P("section", "shard", None),
        P("section", None, "shard"),
    )
    out_specs = (
        P("section", tokens, None),
        P("section", tokens, None),
        P("section", tokens, None),
        P("section", tokens, None),
        P("section", tokens, None),
        P("section", tokens, None),
        P("section", None, tokens),
    )
    return jax.shard_map(shards, mesh=fine, in_specs=in_specs, out_specs=out_specs, check_vma=False)
```

```python
import functools

import jax
import jax.numpy as jnp
import numpy as np
from jax import lax
from jax.experimental import pallas as pl
from jax.experimental.pallas import tpu as pltpu
from jax.sharding import Mesh
from jax.sharding import PartitionSpec as P

D = 960
HEADS = 15
KV_HEADS = 5
GROUP = HEADS // KV_HEADS
HEAD = 64
FF = 2560
QKV = 1600
ROWS = 112
LANES = 128
BLOCKS = 13
EPSILON = 1e-05
ROPE_BASE = 100000.0
NEGATIVE = -1e30
HEAD_SCALE = HEAD ** (-0.5)
BF16 = jnp.bfloat16
F32 = jnp.float32
REP = ("z", "x", "core")
SWAP = [(0, 1), (1, 0)]
VMEM_LIMIT = 12 * 1024 * 1024
OUTER_LIMIT = 20 * 1024 * 1024


def lane_ids(rows):
    return lax.broadcasted_iota(jnp.int32, (rows, LANES), 1)


def swapped_halves(x, low_half):
    return jnp.where(low_half, pltpu.roll(x, LANES - 32, 1), pltpu.roll(x, 32, 1))


def block_of(ref, index, width):
    start = index * LANES
    stop = min(start + LANES, width)
    part = ref[:, start:stop]
    if stop - start < LANES:
        part = jnp.concatenate([part, jnp.zeros((part.shape[0], LANES - (stop - start)), part.dtype)], axis=1)
    return part


def both_halves(block, slot, left):
    if slot == 0:
        low = jnp.where(left, block, 0.0)
        high = pltpu.roll(low, HEAD, 1)
    else:
        high = jnp.where(left, 0.0, block)
        low = pltpu.roll(high, HEAD, 1)
    return low.astype(BF16), high.astype(BF16)


def contract(a, b, dims):
    return lax.dot_general(a, b, ((dims[0:1], dims[1:2]), ((), ())), preferred_element_type=F32)


def attend_kernel(proj_ref, mask_ref, cos_ref, sin_ref, heads_ref, prob_ref, mixed_ref):
    lanes = lane_ids(ROWS)
    left = lanes < HEAD
    low_half = (lanes % HEAD) < 32
    cos = cos_ref[...]
    sin = sin_ref[...]
    mask = mask_ref[0] > 0.0
    blocks = []
    for b in range(BLOCKS):
        x = block_of(proj_ref, b, QKV)
        if b < 10:
            x = x * cos + swapped_halves(x, low_half) * sin
        low = x.astype(BF16)
        blocks.append(low)
        stop = min(b * LANES + LANES, QKV)
        heads_ref[:, b * LANES : stop] = low[:, : stop - b * LANES]
    mixed = [None] * 8
    for kk in range(KV_HEADS):
        kslot, vslot = HEADS + kk, HEADS + KV_HEADS + kk
        keys = both_halves(blocks[kslot // 2].astype(F32), kslot % 2, left)
        values = both_halves(blocks[vslot // 2].astype(F32), vslot % 2, left)
        for h in range(kk * GROUP, kk * GROUP + GROUP):
            half, b = h % 2, h // 2
            scores = contract(keys[half], blocks[b], (1, 1)) * HEAD_SCALE
            scores = jnp.where(mask, scores, NEGATIVE)
            top = jnp.max(scores, axis=0, keepdims=True)
            raised = jnp.exp(scores - top)
            prob = raised / jnp.sum(raised, axis=0, keepdims=True)
            prob_ref[0, h] = prob
            part = contract(prob.astype(BF16), values[half], (0, 0))
            mixed[b] = part if mixed[b] is None else mixed[b] + part
    for b in range(8):
        stop = min(b * LANES + LANES, D)
        mixed_ref[:, b * LANES : stop] = mixed[b].astype(BF16)[:, : stop - b * LANES]


def attend_back_kernel(heads_ref, prob_ref, dmixed_ref, cos_ref, sin_ref, out_ref):
    lanes = lane_ids(ROWS)
    left = lanes < HEAD
    low_half = (lanes % HEAD) < 32
    cos = cos_ref[...]
    sin = sin_ref[...]
    blocks = [block_of(heads_ref, b, QKV) for b in range(BLOCKS)]
    dmixed = [block_of(dmixed_ref, b, D) for b in range(8)]
    outs = [None] * BLOCKS

    def add(index, term):
        outs[index] = term if outs[index] is None else outs[index] + term

    for kk in range(KV_HEADS):
        kslot, vslot = HEADS + kk, HEADS + KV_HEADS + kk
        keys = both_halves(blocks[kslot // 2].astype(F32), kslot % 2, left)
        values = both_halves(blocks[vslot // 2].astype(F32), vslot % 2, left)
        dkeys = [None, None]
        dvalues = [None, None]
        for h in range(kk * GROUP, kk * GROUP + GROUP):
            half, b = h % 2, h // 2
            prob = prob_ref[0, h]
            dprob = contract(values[half], dmixed[b], (1, 1))
            inner = jnp.sum(dprob * prob, axis=0, keepdims=True)
            dscore = (prob * (dprob - inner)).astype(BF16)
            add(b, contract(dscore, keys[half], (0, 0)))
            dk = contract(dscore, blocks[b], (1, 0))
            dv = contract(prob.astype(BF16), dmixed[b], (1, 0))
            dkeys[half] = dk if dkeys[half] is None else dkeys[half] + dk
            dvalues[half] = dv if dvalues[half] is None else dvalues[half] + dv
        for slot, (low, high) in ((kslot, dkeys), (vslot, dvalues)):
            low = jnp.where(left, low, 0.0)
            high = jnp.where(left, 0.0, high)
            if slot % 2 == 0:
                term = low + pltpu.roll(high, HEAD, 1)
            else:
                term = pltpu.roll(low, HEAD, 1) + high
            add(slot // 2, term)
    for b in range(BLOCKS):
        x = outs[b]
        if b < 10:
            x = x * HEAD_SCALE
            x = x * cos - swapped_halves(x, low_half) * sin
        stop = min(b * LANES + LANES, QKV)
        out_ref[:, b * LANES : stop] = x.astype(BF16)[:, : stop - b * LANES]


def row_spec(width):
    return pl.BlockSpec((ROWS, width), lambda i: (i, 0))


def attend(projected, mask, cos, sin):
    count = mask.shape[0]
    rows = count * ROWS
    return pl.pallas_call(
        attend_kernel,
        grid=(count,),
        in_specs=[
            row_spec(QKV),
            pl.BlockSpec((1, ROWS, ROWS), lambda i: (i, 0, 0)),
            row_spec(LANES),
            row_spec(LANES),
        ],
        out_specs=[
            row_spec(QKV),
            pl.BlockSpec((1, HEADS, ROWS, ROWS), lambda i: (i, 0, 0, 0)),
            row_spec(D),
        ],
        out_shape=[
            jax.ShapeDtypeStruct((rows, QKV), BF16),
            jax.ShapeDtypeStruct((count, HEADS, ROWS, ROWS), F32),
            jax.ShapeDtypeStruct((rows, D), BF16),
        ],
        compiler_params=pltpu.CompilerParams(vmem_limit_bytes=VMEM_LIMIT),
        name="attend",
    )(projected, mask, cos, sin)


def attend_back(heads, prob, dmixed, cos, sin):
    count = prob.shape[0]
    rows = count * ROWS
    return pl.pallas_call(
        attend_back_kernel,
        grid=(count,),
        in_specs=[
            row_spec(QKV),
            pl.BlockSpec((1, HEADS, ROWS, ROWS), lambda i: (i, 0, 0, 0)),
            row_spec(D),
            row_spec(LANES),
            row_spec(LANES),
        ],
        out_specs=row_spec(QKV),
        out_shape=jax.ShapeDtypeStruct((rows, QKV), BF16),
        compiler_params=pltpu.CompilerParams(vmem_limit_bytes=VMEM_LIMIT),
        name="attend_back",
    )(heads, prob, dmixed, cos, sin)


def tables(segments):
    count, rows = segments.shape
    earlier = jnp.sum((segments[:, None, :] < segments[:, :, None]).astype(jnp.int32), axis=2)
    position = (jnp.arange(rows, dtype=jnp.int32)[None, :] - earlier).astype(F32).reshape(count * rows, 1)
    frequency = ROPE_BASE ** (-jnp.arange(HEAD // 2, dtype=F32) * 2.0 / HEAD)
    angles = position * frequency[None, :]
    cos, sin = jnp.cos(angles), jnp.sin(angles)
    order = jnp.arange(rows, dtype=jnp.int32)
    mask = (segments[:, :, None] == segments[:, None, :]) & (order[:, None] <= order[None, :])[None]
    return (
        jnp.concatenate([cos] * 4, axis=1),
        jnp.concatenate([-sin, sin, -sin, sin], axis=1),
        mask.astype(F32),
    )


def mm(a, b):
    return jnp.dot(a, b, preferred_element_type=F32)


def mmt(a, b):
    return lax.dot_general(a, b, (((1,), (1,)), ((), ())), preferred_element_type=F32)


def layer_forward(stream, gains, weights, table, mm_out=mm, mm_gateup=mm, then=lambda mixed: mixed, mm_down=mmt):
    cos, sin, mask = table
    first_scale = lax.rsqrt(jnp.mean(stream * stream, axis=-1, keepdims=True) + EPSILON)
    attn_norm = (stream * first_scale * gains[0]).astype(BF16)
    projected = mm(attn_norm, weights[0])
    heads, prob, mixed = attend(projected, mask, cos, sin)
    mixed = then(mixed)
    middle = stream + mm_out(mixed, weights[1])
    second_scale = lax.rsqrt(jnp.mean(middle * middle, axis=-1, keepdims=True) + EPSILON)
    ffn_norm = (middle * second_scale * gains[1]).astype(BF16)
    gateup = mm_gateup(ffn_norm, weights[2])
    gate, up = gateup[:, :FF], gateup[:, FF:]
    hidden = (gate * jax.nn.sigmoid(gate) * up).astype(BF16)
    output = middle + mm_down(hidden, weights[3])
    return output, (stream, first_scale, attn_norm, heads, prob, mixed, middle, second_scale, ffn_norm, gate, up, hidden)


def norm_back(incoming, gain, scale, normed):
    scaled = incoming * gain
    return scale * (scaled - normed * jnp.mean(scaled * normed, axis=-1, keepdims=True))


def layer_backward(dy, kept, gains, weights, table, grads):
    qkv_w, out_w, gateup_w, down_w = weights
    cos, sin, _ = table
    stream, first_scale, attn_norm, heads, prob, mixed, middle, second_scale, ffn_norm, gate, up, hidden = kept
    dz = dy.astype(BF16)
    dhidden = mm(dz, down_w)
    s = jax.nn.sigmoid(gate)
    dgateup = jnp.concatenate(
        [dhidden * up * s * (1.0 + gate * (1.0 - s)), dhidden * gate * s], axis=1
    ).astype(BF16)
    if grads is not None:
        grads.down(dz)
        made = grads.gateup(dgateup)
    dffn = mmt(dgateup, gateup_w)
    second_normed = middle * second_scale
    dmiddle = dy + norm_back(dffn, gains[1], second_scale, second_normed)
    dbranch = dmiddle.astype(BF16)
    if grads is not None:
        grads.branch(dbranch)
        dbranch, _ = lax.optimization_barrier((dbranch, made))
    dmixed = mmt(dbranch, out_w).astype(BF16)
    dprojected = attend_back(heads, prob, dmixed, cos, sin)
    if grads is not None:
        dprojected = grads.heads(dprojected)
    dattn = mmt(dprojected, qkv_w)
    first_normed = stream * first_scale
    if grads is not None:
        gain_grads = jnp.stack([jnp.sum(dattn * first_normed, axis=0), jnp.sum(dffn * second_normed, axis=0)])
        grads.attention(gain_grads)
    return dmiddle + norm_back(dattn, gains[0], first_scale, first_normed)


def place_kernel(counts, at_ref, *refs):
    out_ref = refs[-1]
    step = pl.program_id(0)
    first = 0
    for ref, count in zip(refs, counts):

        @pl.when((step >= first) & (step < first + count))
        def _(ref=ref):
            out_ref[...] = ref[...]

        first += count


def placed(pieces, counts, at, block, shape, base=None):
    firsts = np.cumsum([0] + list(counts))
    bases = () if base is None else (base,)

    def piece_spec(p):
        start, count = int(firsts[p]), counts[p]
        return pl.BlockSpec(block, lambda i, at_ref: (jnp.clip(i - start, 0, count - 1), 0))

    return pl.pallas_call(
        functools.partial(place_kernel, counts),
        grid_spec=pltpu.PrefetchScalarGridSpec(
            num_scalar_prefetch=1,
            grid=(int(firsts[-1]),),
            in_specs=[piece_spec(p) for p in range(len(pieces))] + [pl.BlockSpec(memory_space=pl.ANY)] * len(bases),
            out_specs=pl.BlockSpec(block, lambda i, at_ref: (at_ref[0, i], at_ref[1, i])),
        ),
        out_shape=jax.ShapeDtypeStruct(shape, BF16),
        compiler_params=pltpu.CompilerParams(vmem_limit_bytes=VMEM_LIMIT),
        input_output_aliases={1 + len(pieces): 0} if bases else {},
        name="placed",
    )(jnp.stack(at).astype(jnp.int32), *pieces, *bases)


def hidden_outer_kernel(l0_ref, r0_ref, l1_ref, r1_ref, out_ref, total):
    step = pl.program_id(0)

    @pl.when(step == 0)
    def _():
        for s in range(2):
            part = slice(s * (FF // 2), (s + 1) * (FF // 2))
            value = contract(l0_ref[:, part], r0_ref[...], (0, 0)) + contract(l1_ref[:, part], r1_ref[...], (0, 0))
            total[part] = jnp.concatenate([value, jnp.zeros((FF // 2, 32), F32)], axis=1)

    def rows(s, chunk, start, stop):
        at = s * (FF // 2) + chunk * 80
        return total[at + start : at + stop]

    for j in range(3):

        @pl.when(step == j)
        def _(j=j):
            for chunk in range(16):
                if j == 0:
                    group = rows(0, chunk, 0, 64)
                elif j == 1:
                    group = jnp.concatenate([rows(0, chunk, 64, 80), rows(1, chunk, 0, 48)], axis=0)
                else:
                    group = jnp.concatenate([rows(1, chunk, 48, 80), jnp.zeros((32, 512), F32)], axis=0)
                out_ref[chunk * 64 : chunk * 64 + 64] = group.astype(BF16)


def hidden_outer(left, right):
    operands = (left[0], right[0], left[1], right[1])
    return pl.pallas_call(
        hidden_outer_kernel,
        grid=(3,),
        in_specs=[pl.BlockSpec(a.shape, lambda i: (0, 0)) for a in operands],
        out_specs=pl.BlockSpec((1024, 512), lambda i: (0, 5 + i)),
        out_shape=jax.ShapeDtypeStruct((1024, FF + 1536), BF16),
        scratch_shapes=[pltpu.VMEM((FF, 512), F32)],
        compiler_params=pltpu.CompilerParams(vmem_limit_bytes=OUTER_LIMIT),
        name="hidden_outer",
    )(*operands)


def gateup_outer_kernel(l0_ref, r0_ref, l1_ref, r1_ref, base_ref, out_ref):
    total = contract(l0_ref[...], r0_ref[...], (0, 0)) + contract(l1_ref[...], r1_ref[...], (0, 0))
    out_ref[...] = total.astype(BF16)


def gateup_outer(left, right, base):
    rows, tile = left[0].shape[0], 256
    left_spec = pl.BlockSpec((rows, tile), lambda i: (0, i))
    right_spec = pl.BlockSpec((rows, FF), lambda i: (0, 0))
    return pl.pallas_call(
        gateup_outer_kernel,
        grid=(1024 // tile,),
        in_specs=[left_spec, right_spec, left_spec, right_spec, pl.BlockSpec(memory_space=pl.ANY)],
        out_specs=pl.BlockSpec((tile, FF), lambda i: (i, 0)),
        out_shape=jax.ShapeDtypeStruct(base.shape, BF16),
        input_output_aliases={4: 0},
        compiler_params=pltpu.CompilerParams(vmem_limit_bytes=OUTER_LIMIT),
        name="gateup_outer",
    )(left[0], right[0], left[1], right[1], base)


def attention_outer_kernel(m0, b0, m1, b1, a0, p0, a1, p1, pick_ref, gain_ref, out_ref):
    first = contract(m0[...], b0[...], (0, 0)) + contract(m1[...], b1[...], (0, 0))
    second = contract(a0[...], p0[...], (0, 0)) + contract(a1[...], p1[...], (0, 0))
    out_ref[:, :1280] = jnp.concatenate([first, second], axis=1).astype(BF16)
    out_ref[:, 1280:] = contract(pick_ref[...], gain_ref[...], (0, 1)).astype(BF16)


def attention_outer(mixed, dbranch, attn, dprojected, pick, gain_grads):
    rows, depth = mixed[0].shape
    tile = 256

    def left(height):
        return pl.BlockSpec((height, tile), lambda i: (0, i))

    def right(height, width):
        return pl.BlockSpec((height, width), lambda i: (0, 0))

    return pl.pallas_call(
        attention_outer_kernel,
        grid=(depth // tile,),
        in_specs=[left(rows), right(rows, 480)] * 2 + [left(rows), right(rows, 800)] * 2
        + [left(D), right(LANES, D)],
        out_specs=pl.BlockSpec((tile, 1280 + LANES), lambda i: (i, 0)),
        out_shape=jax.ShapeDtypeStruct((depth, 1280 + LANES), BF16),
        compiler_params=pltpu.CompilerParams(vmem_limit_bytes=OUTER_LIMIT),
        name="attention_outer",
    )(mixed[0], dbranch[0], mixed[1], dbranch[1], attn[0], dprojected[0], attn[1], dprojected[1], pick, gain_grads)


class Ring:
    def __init__(self, v, axis, dim):
        self.v, self.axis, self.dim = v, axis, dim
        self.me = lax.axis_index(axis)
        far, after, ahead = self.part(2), self.part(1), self.part(3)
        cut = self.cut = far.shape[0] // 2
        self.low = self.up(jnp.concatenate([far[:cut], after[cut:]], axis=0))
        self.high = self.back(jnp.concatenate([far[cut:], ahead[:cut]], axis=0))

    def up(self, x):
        return lax.ppermute(x, self.axis, [(i, (i + 1) % 4) for i in range(4)])

    def back(self, x):
        return lax.ppermute(x, self.axis, [(i, (i + 3) % 4) for i in range(4)])

    def part(self, step):
        return lax.dynamic_index_in_dim(self.v, (self.me + step) % 4, self.dim, keepdims=False)

    def end(self, dep):
        self.low_end, self.high_end, dep = lax.optimization_barrier((self.low_end, self.high_end, dep))
        return dep

    def passed(self):
        cut = self.cut
        return self.part(1)[:cut] + self.low[:cut], self.part(3)[cut:] + self.high[:cut]

    def second(self, passed):
        self.low_end, self.high_end = self.up(passed[0]), self.back(passed[1])

    def last(self):
        cut, own = self.cut, self.part(0).astype(F32)
        low = own[:cut] + self.low_end.astype(F32) + self.high[cut:].astype(F32)
        high = own[cut:] + self.high_end.astype(F32) + self.low[cut:].astype(F32)
        return jnp.concatenate([low, high], axis=0).astype(BF16)


def row_order():
    pick = np.zeros((D, 1024), np.float32)
    for row in range(D):
        s, rest = divmod(row, 480)
        chunk, i = divmod(rest, 30)
        pick[row, chunk * 64 + s * 32 + i] = 1.0
    return pick


def with_other(x):
    return x, lax.ppermute(x, "core", SWAP)


def owned_kernel(core_ref, own_ref, across_ref, beside_ref, corner_ref, gateup_ref, output_ref, qkv_ref, down_ref, gains_ref):
    here = own_ref[...].astype(F32) + across_ref[...].astype(F32)
    there = beside_ref[...].astype(F32) + corner_ref[...].astype(F32)
    first = core_ref[0] == 0
    low = jnp.where(first, here, there)
    high = jnp.where(first, there, here)

    def columns(start, width, rows):
        return jnp.concatenate([low[:rows, start : start + width], high[:rows, start : start + width]], axis=1)

    gateup_ref[:, 0, :] = columns(0, FF, 15)
    output_ref[:, 0, :] = columns(FF, 480, 15)
    qkv_ref[:, 0, :] = columns(FF + 480, 800, 15)
    at = FF + 1280
    gains_ref[...] = low[:, at : at + LANES] + high[:, at : at + LANES]
    at += LANES
    for j, rows in enumerate((16, 16, 8)):
        down_ref[16 * j : 16 * j + rows] = columns(at + 512 * j, 480, rows)


def owned(core, *parts):
    vmem = pl.BlockSpec(memory_space=pltpu.VMEM)
    shapes = [(15, 1, 2 * FF), (15, 1, D), (15, 1, QKV), (40, D), (16, LANES)]
    return pl.pallas_call(
        owned_kernel,
        in_specs=[pl.BlockSpec(memory_space=pltpu.SMEM)] + [vmem] * 4,
        out_specs=[vmem] * 5,
        out_shape=[jax.ShapeDtypeStruct(shape, F32) for shape in shapes],
        compiler_params=pltpu.CompilerParams(vmem_limit_bytes=VMEM_LIMIT),
        name="owned",
    )(core.reshape(1).astype(jnp.int32), *parts)


class Gradients:
    def __init__(self, kept):
        self.core = lax.axis_index("core") == 0
        self.shard = lax.axis_index("shard") == 0
        self.pick = jnp.asarray(row_order(), BF16)
        attn_norm, mixed, ffn_norm, hidden = kept[2], kept[5], kept[8], kept[11]
        self.hidden = with_other(hidden)
        self.ffn = with_other(mm(ffn_norm, self.pick).astype(BF16))
        self.attn = with_other(mm(attn_norm, self.pick).astype(BF16))
        self.mixed = with_other(mm(mixed, self.pick).astype(BF16))

    def ready(self, dep):
        ffn, attn, mixed = self.ffn[0], self.attn[0], self.mixed[0]
        ffn, attn, mixed, dep = lax.optimization_barrier((ffn, attn, mixed, dep))
        self.ffn, self.attn, self.mixed = (ffn, self.ffn[1]), (attn, self.attn[1]), (mixed, self.mixed[1])
        return dep

    def shared(self, right):
        cut = right.shape[1] // 2
        keep = jnp.where(self.core, right[:, :cut], right[:, cut:])
        give = jnp.where(self.core, right[:, cut:], right[:, :cut])
        return keep, lax.ppermute(give, "core", SWAP)

    def joined(self, parts):
        shard, core = lax.axis_index("shard"), lax.axis_index("core")
        axes = ("shard", "core")

        def part(s, c):
            return lax.dynamic_index_in_dim(parts, 2 * s + c, 0, keepdims=False)

        across = lax.ppermute(part(1 - shard, core), axes, [(0, 2), (2, 0), (1, 3), (3, 1)])
        beside = lax.ppermute(part(shard, 1 - core), axes, [(0, 1), (1, 0), (2, 3), (3, 2)])
        corner = lax.ppermute(part(1 - shard, 1 - core), axes, [(0, 3), (3, 0), (1, 2), (2, 1)])
        return owned(core, part(shard, core), across, beside, corner)

    def down(self, dz):
        self.base = hidden_outer(self.hidden, self.shared(dz))

    def gateup(self, dgateup):
        made = gateup_outer(self.ffn, self.shared(dgateup), self.base)
        self.ffn_piece = lax.psum_scatter(made, ("z", "x"), scatter_dimension=0, tiled=True)
        return made

    def branch(self, dbranch):
        self.dbranch = self.shared(dbranch)

    def heads(self, dprojected):
        self.dprojected = self.shared(dprojected)
        return dprojected

    def attention(self, gain_grads):
        gain_grads = jnp.pad(gain_grads.astype(BF16), ((0, LANES - 2), (0, 0)))
        made = attention_outer(self.mixed, self.dbranch, self.attn, self.dprojected, self.pick, gain_grads)
        width = made.shape[1]
        attention = Ring(made.reshape(4, 4, 64, width), "z", 0)
        attention.second(attention.passed())
        attention = Ring(attention.last(), "x", 0)
        attention.second(attention.passed())
        self.ffn_piece = attention.end(self.ffn_piece)
        self.attention_piece = attention.last()

    def finish(self):
        def by_owner(piece):
            piece = piece.reshape(2, 32, piece.shape[1])
            both = jnp.stack([piece[:, :16], piece[:, 15:31]], axis=1)
            return both.reshape(4, 16, piece.shape[2])

        groups = [self.ffn_piece[:, FF + 512 * j : FF + 512 * j + 512] for j in range(3)]
        tail = jnp.concatenate(groups, axis=0)[:160].reshape(4, 40, 512)
        tail = jnp.pad(tail, ((0, 0), (0, 8), (0, 0)))
        parts = jnp.concatenate(
            [by_owner(self.ffn_piece[:, :FF]), by_owner(self.attention_piece)]
            + [tail[:, 16 * i : 16 * i + 16] for i in range(3)],
            axis=2,
        )
        gateup, output, qkv, down, gains = self.joined(parts)
        flat = lambda a: a.reshape(1, 15, a.shape[2])
        return flat(qkv), flat(output), flat(gateup), down[None], gains[:15, :2].T[None]


def shards(tokens, segments, cotangent, qkv_weight, output_weight, gateup_weight, down_weight, norm_gains):
    leading = lax.axis_index("section") == 0
    first = lax.axis_index("shard") == 0
    rep = lax.axis_index(REP)

    core = lax.axis_index("core")
    shard = lax.axis_index("shard")
    own_out, own_gateup = output_weight[0], gateup_weight[0]
    rows = jnp.concatenate(
        [lax.dynamic_slice_in_dim(w, jnp.minimum(rep * 16, 464), 16, 0) for w in (own_gateup, own_out)], axis=1
    )
    others = lax.all_gather(lax.ppermute(rows, "shard", SWAP), REP, axis=0, tiled=True)
    own_gains = norm_gains[0]
    other_gains = lax.ppermute(own_gains, "shard", SWAP)
    gains = jnp.concatenate(
        [jnp.where(first, own_gains, other_gains), jnp.where(first, other_gains, own_gains)], axis=1
    ).astype(F32)

    def sent(own):
        half = own.shape[0] // 2
        return lax.ppermute(lax.dynamic_slice_in_dim(own, core * half, half, 0), "shard", SWAP)

    def whole(own, got):
        half, width = got.shape
        beside = lax.ppermute(got, "core", SWAP)
        place = 2 * (1 - shard)
        at = jnp.stack([2 * shard, 2 * shard + 1, place + core, place + 1 - core])
        return placed((own, got, beside), (2, 1, 1), (at, at * 0), (half, width), (4 * half, width))

    def own_turned(own):
        depth, width = own.shape
        rows = jnp.arange(4)
        return placed((own,), (4,), (rows, rows * 0 + shard), (depth // 4, width), (depth, 2 * width))

    def whole_turned(base, got, beside):
        half, width = got.shape
        rows = jnp.stack([2 * core, 2 * core + 1, 2 - 2 * core, 3 - 2 * core])
        return placed((got, beside), (2, 2), (rows, rows * 0 + 1 - shard), (half // 2, width), base.shape, base)

    def own_first(own, rows):
        at = shard * (480 // rows) + jnp.arange(480 // rows)
        return placed((own,), (480 // rows,), (at, at * 0), (rows, own.shape[1]), (D, own.shape[1]))

    def beside_own(base, other, rows):
        at = (1 - shard) * (480 // rows) + jnp.arange(480 // rows)
        return placed((other,), (480 // rows,), (at, at * 0), (rows, base.shape[1]), base.shape, base)

    def halved(x, pieces):
        cut = D // 2
        own = jnp.where(first, x[:, :cut], x[:, cut:])
        other = jnp.pad(jnp.where(first, x[:, cut:], x[:, :cut]), ((0, 0), (0, 32)))
        return mm(own, pieces[0]) + mm(other, pieces[1])

    turned = down_weight[0].T
    coming = [sent(qkv_weight[0]), sent(turned)]
    qkv_w = whole(qkv_weight[0], coming[0])

    table = tables(segments)
    inputs = tokens.astype(F32)
    down_base, out_base, gateup_base = own_turned(turned), own_first(own_out, 240), own_first(own_gateup, 80)
    parts = [qkv_w, (own_out, others[:, 2 * FF :]), (own_gateup, others[:, : 2 * FF]), None]

    def fetch_down(mixed):
        mixed, got = lax.optimization_barrier((mixed, coming[1]))
        parts[3] = (got, lax.ppermute(got, "core", SWAP))
        return mixed

    def down_pieces(hidden, pieces):
        cut, one = FF // 2, core == 0
        own = jnp.where(first, hidden[:, :cut], hidden[:, cut:])
        other = jnp.where(first, hidden[:, cut:], hidden[:, :cut])
        got, beside = mmt(other, pieces[0]), mmt(other, pieces[1])
        return mmt(own, turned) + jnp.concatenate([jnp.where(one, got, beside), jnp.where(one, beside, got)], axis=1)

    early, _ = layer_forward(inputs, gains, parts, table, halved, halved, fetch_down, down_pieces)
    early = early.astype(BF16)
    arrived = lax.ppermute(early, "section", [(0, 1)])
    _, others, pieces = lax.optimization_barrier((early, others, parts[3]))
    weights = (qkv_w, beside_own(out_base, others[:, 2 * FF :], 240), beside_own(gateup_base, others, 80), whole_turned(down_base, *pieces))
    arrived, weights = lax.optimization_barrier((arrived, weights))
    arrived = arrived.astype(F32)
    stream = jnp.where(leading, inputs, arrived)
    output, kept = layer_forward(stream, gains, weights, table)

    early = layer_backward(cotangent, kept, gains, weights, table, None).astype(BF16)
    arrived = lax.ppermute(early, "section", [(1, 0)])
    _, kept = lax.optimization_barrier((early, kept))
    grads = Gradients(kept)
    arrived = grads.ready(arrived).astype(F32)
    dy = lax.optimization_barrier(jnp.where(leading, arrived, cotangent))
    down = layer_backward(dy, kept, gains, weights, table, grads)
    return (output[None], down[None], *grads.finish())


def solution(mesh):
    sizes = mesh.shape
    fine = Mesh(
        mesh.devices.reshape(sizes["section"], sizes["shard"], 4, 4, 2),
        ("section", "shard", "z", "x", "core"),
    )
    tokens = ("shard",) + REP
    in_specs = (
        P(tokens, None),
        P(tokens, None),
        P(tokens, None),
        P("section", "shard", None),
        P("section", "shard", None),
        P("section", "shard", None),
        P("section", "shard", None),
        P("section", None, "shard"),
    )
    out_specs = (
        P("section", tokens, None),
        P("section", tokens, None),
        P("section", tokens, None),
        P("section", tokens, None),
        P("section", tokens, None),
        P("section", tokens, None),
        P("section", None, tokens),
    )
    return jax.shard_map(shards, mesh=fine, in_specs=in_specs, out_specs=out_specs, check_vma=False)
```
